128 devices in a mesh: row: 8 (over z, core), col: 16 (over x, y).
Axes of the slice: x: 4, y: 4, z: 4, core: 2. Of those that a mesh axis runs over, the one named last changes fastest.
Arguments:
- context: bfloat16 [1024, 6144], P('col', 'row'), may hold values from -3 to 3
- residual: bfloat16 [1024, 12288], P('row', 'col'), may hold values from -80 to 80
- norm_gain: float32 [12288], P('col'), may hold values from 0.1 to 1.9
- w_out: bfloat16 [6144, 12288], P('row', 'col'), may hold values from -0.078125 to 0.078125
- w_up: bfloat16 [12288, 24576], P('col', 'row'), may hold values from -4 to 4
- w_down: bfloat16 [24576, 12288], P('row', 'col'), may hold values from -0.0390625 to 0.0390625
- upstream: bfloat16 [1024, 12288], P('row', 'col'), may hold values from -6 to 6
Outputs:
- grad_residual: bfloat16 [1024, 12288], P('row', 'col')
- grad_context: bfloat16 [1024, 6144], P('col', 'row')
- grad_gain: float32 [12288], P('col')
- grad_w_out: bfloat16 [6144, 12288], P('row', 'col')
- grad_w_up: bfloat16 [12288, 24576], P('col', 'row')
- grad_w_down: bfloat16 [24576, 12288], P('row', 'col')
The draws below stay inside these ranges and needn't reach their ends.
All inputs are finite; a program needn't handle non-finite values.
Results may differ from the reference program's by a relative error of at most 0.029.
Values may be sent and summed in bfloat16 or wider, within the bound.
A program may use at most 128 MiB of HBM per device.

```python
import math
import jax
import jax.numpy as jnp
from jax import lax

D = 12288
FF = 24576
HD = 6144
TOKENS = 1024
N_COL = 16


def draw_residual(key, part):
    key = jax.random.fold_in(key, 7)
    key_base, key_rows, key_cols, key_offset, key_sign = jax.random.split(key, 5)
    position = jnp.arange(D, dtype=jnp.float32) / D
    sign = jnp.where(jax.random.bernoulli(key_sign, 0.5, (TOKENS, 1)), 1.0, -1.0)
    base = jnp.clip(jax.random.normal(key_base, (TOKENS, D), jnp.float32), -4.0, 4.0)
    row_scale = jnp.exp(jax.random.uniform(key_rows, (TOKENS, 1), jnp.float32, math.log(0.5), math.log(5.0)))
    col_scale = jnp.exp(jax.random.uniform(key_cols, (D,), jnp.float32, math.log(0.2), math.log(2.0))) * jnp.exp(position * math.log(3.0))
    offset_size = jax.random.uniform(key_offset, (TOKENS, 1), jnp.float32, 0.5, 2.0)
    ramp = 0.4 * jnp.exp(position * math.log(6.0))
    return (0.5 * base * row_scale * col_scale + sign * offset_size * ramp).astype(jnp.bfloat16)


def draw_w_up(key, part):
    key = jax.random.fold_in(key, 11)
    key_base, key_rise, key_common = jax.random.split(key, 3)
    position = jnp.arange(D, dtype=jnp.float32) / D
    common = jnp.clip(jax.random.normal(key_common, (FF,), jnp.float32), -3.0, 3.0)
    base = jnp.clip(jax.random.normal(key_base, (D, FF), jnp.float32), -4.0, 4.0)
    rise = 0.3 * jnp.exp(position * math.log(10.0)) * jax.random.uniform(key_rise, (D,), jnp.float32, 0.5, 1.5)
    value = base / math.sqrt(D) + 0.03 * rise[:, None] * common[None, :] / math.sqrt(FF)
    return value.astype(jnp.bfloat16)


def shard_levels(own_key, dims, cuts, least, high):
    level, own = 1.0, jax.random.fold_in(own_key, 6)
    for axis_at, blocks in cuts:
        steps = jnp.exp(jax.random.uniform(jax.random.fold_in(own, axis_at), (blocks,), jnp.float32, least / len(cuts), high / len(cuts)))
        level = level * jnp.repeat(steps, dims[axis_at] // blocks).reshape([-1 if axis == axis_at else 1 for axis in range(len(dims))])
    return level


def normal_values(rng, shape, scale, most, shards=(), kind=jnp.bfloat16):
    drawn = scale * jax.random.normal(rng, shape, jnp.float32)
    if shards:
        drawn = drawn * shard_levels(rng, shape, shards, -0.22, 0.18)
    return jnp.clip(drawn, -most, most).astype(kind)


def setup_inputs(seed: int = 0) -> dict:
    splits = jax.random.split(jax.random.key(seed), 8)
    context = normal_values(splits[0], (TOKENS, HD), 0.5, 3.0, ((0, 16), (1, 8)))
    residual = draw_residual(jax.random.fold_in(splits[7], 71), 0)
    norm_gain = jnp.clip(1.0 + 0.18 * jax.random.normal(splits[2], (D,), jnp.float32), 0.1, 1.9)
    w_out = normal_values(splits[3], (HD, D), HD ** -0.5, 0.078125, ((0, 8), (1, 16)))
    w_up = draw_w_up(jax.random.fold_in(splits[7], 71), 0)
    w_down = normal_values(splits[5], (FF, D), FF ** -0.5, 0.0390625, ((0, 8), (1, 16)))
    upstream = normal_values(splits[6], (TOKENS, D), 1.0, 6.0, ((0, 8), (1, 16)))
    return {"context": context, "residual": residual, "norm_gain": norm_gain, "w_out": w_out, "w_up": w_up, "w_down": w_down, "upstream": upstream}


def gelu_value(values):
    tanh_arg = 0.7978845608028654 * (values + 0.044715 * values * values * values)
    return 0.5 * values * (1.0 + jnp.tanh(tanh_arg))

def gelu_slope(values):
    tanh_val = jnp.tanh(0.7978845608028654 * (values + 0.044715 * values * values * values))
    return 0.5 * (1.0 + tanh_val) + 0.5 * values * (1.0 - tanh_val * tanh_val) * 0.7978845608028654 * (1.0 + 0.134145 * values * values)

def blocked_sum(operand, weights):
    row_count = operand.shape[0]
    block_width = operand.shape[1] // N_COL
    operand_blocks = operand.reshape(row_count, N_COL, block_width).transpose(1, 0, 2)
    weight_blocks = weights.reshape(N_COL, block_width, weights.shape[1])

    def add_block(carried, blocks):
        partial_sum = jnp.dot(blocks[0], blocks[1], preferred_element_type=jnp.float32)
        rounded = lax.optimization_barrier(partial_sum.astype(jnp.bfloat16))
        return (carried + rounded.astype(jnp.float32), None)
    start_sum = jnp.zeros((row_count, weights.shape[1]), jnp.float32)
    result, unused = lax.scan(add_block, start_sum, (operand_blocks, weight_blocks))
    return result

def contract_rows(first_op, second_op):
    return lax.dot_general(first_op, second_op, (((0,), (0,)), ((), ())), preferred_element_type=jnp.float32)

def reference(context, residual, norm_gain, w_out, w_up, w_down, upstream):
    attended = jnp.dot(context, w_out, preferred_element_type=jnp.float32)
    summed = residual.astype(jnp.float32) + attended
    row_mean = lax.optimization_barrier(jnp.mean(summed, axis=1, keepdims=True))
    centered = summed - row_mean
    row_var = lax.optimization_barrier(jnp.mean(centered * centered, axis=1, keepdims=True))
    inv_std = lax.rsqrt(row_var + 1e-05)
    unit_rows = centered * inv_std
    normed = (unit_rows * norm_gain).astype(jnp.bfloat16)
    hidden_pre = blocked_sum(normed, w_up)
    activated = gelu_value(hidden_pre).astype(jnp.bfloat16)
    grad_w_down = contract_rows(activated, upstream).astype(jnp.bfloat16)
    grad_act = blocked_sum(upstream, w_down.T)
    grad_pre = (grad_act * gelu_slope(hidden_pre)).astype(jnp.bfloat16)
    grad_w_up = contract_rows(normed, grad_pre).astype(jnp.bfloat16)
    grad_normed = jnp.dot(grad_pre, w_up.T, preferred_element_type=jnp.float32)
    grad_gain = lax.optimization_barrier(jnp.sum(grad_normed * unit_rows, axis=0))
    scaled = grad_normed * norm_gain
    mean_scaled = lax.optimization_barrier(jnp.mean(scaled, axis=1, keepdims=True))
    mean_aligned = lax.optimization_barrier(jnp.mean(scaled * unit_rows, axis=1, keepdims=True))
    grad_residual = (upstream.astype(jnp.float32) + inv_std * (scaled - mean_scaled - unit_rows * mean_aligned)).astype(jnp.bfloat16)
    grad_w_out = contract_rows(context, grad_residual).astype(jnp.bfloat16)
    grad_context = blocked_sum(grad_residual, w_out.T).astype(jnp.bfloat16)
    return (grad_residual, grad_context, grad_gain, grad_w_out, grad_w_up, grad_w_down)
```

```python
import jax
import jax.numpy as jnp
from jax import lax
from jax.experimental import pallas as pl
from jax.experimental.pallas import tpu as pltpu
from jax.sharding import PartitionSpec as P

MESH = pl.DeviceIdType.MESH
BF16 = jnp.bfloat16
F32 = jnp.float32
D = 12288
W = 768
PAIRS = 6
C = 256
CH = 384
ACT_DELAY = 6
TICKS = 28


def gelu_parts(values):
    tanh_val = jnp.tanh(0.7978845608028654 * (values + 0.044715 * values * values * values))
    value = 0.5 * values * (1.0 + tanh_val)
    slope = 0.5 * (1.0 + tanh_val) + 0.5 * values * (
        1.0 - tanh_val * tanh_val
    ) * 0.7978845608028654 * (1.0 + 0.134145 * values * values)
    return value, slope


def dot(first_op, second_op):
    return jnp.dot(first_op, second_op, preferred_element_type=F32)


def dot_cols(first_op, second_op):
    return lax.dot_general(
        first_op, second_op, (((1,), (1,)), ((), ())), preferred_element_type=F32
    )


class Ring:
    def __init__(self, place, device):
        self.place = place
        self.right = lax.rem(place + 1, 4)
        self.opposite = lax.rem(place + 2, 4)
        self.left = lax.rem(place + 3, 4)
        self.device = device


def remote(src, dst, send, recv, device):
    return pltpu.make_async_remote_copy(
        src_ref=src, dst_ref=dst, send_sem=send, recv_sem=recv, device_id=device, device_id_type=MESH
    )


class Copies:
    def __init__(self, make, count):
        self.make, self.count = make, count

    def __getitem__(self, k):
        return self.make(k)

    def __iter__(self):
        return (self.make(k) for k in range(self.count))


class Scatter:
    def __init__(self, ring, half, landing, send, recv):
        r, l, o = ring.right, ring.left, ring.opposite
        plan = [(o, 0, r), (r, 1, r), (r, 0, r), (o, 1, l), (l, 0, l), (l, 1, l)]
        self.ring, self.half, self.landing = ring, half, landing

        def make(k):
            i, h, to = plan[k]
            return remote(half(i, h), landing.at[k], send.at[k], recv.at[k], ring.device(to))

        self.copies = Copies(make, 6)

    def start(self):
        for k in (0, 3, 1, 4):
            self.copies[k].start()

    def middle(self):
        for k, i, h, nxt in ((0, self.ring.right, 0, 2), (3, self.ring.left, 1, 5)):
            self.copies[k].wait_recv()
            part = self.half(i, h)
            part[...] = (part[...].astype(F32) + self.landing[k].astype(F32)).astype(BF16)
            self.copies[nxt].start()

    def finish(self):
        for k in (1, 4, 2, 5):
            self.copies[k].wait_recv()
        for copy in self.copies:
            copy.wait_send()
        me = self.ring.place
        first = (
            self.half(me, 0)[...].astype(F32)
            + self.landing[2].astype(F32)
            + self.landing[4].astype(F32)
        )
        second = (
            self.half(me, 1)[...].astype(F32)
            + self.landing[1].astype(F32)
            + self.landing[5].astype(F32)
        )
        return first, second


class Gather:
    def __init__(self, ring, group, half, send, recv):
        r, l = ring.right, ring.left
        me = ring.place

        def make(k):
            ref = (lambda: group(me), lambda: group(me), lambda: half(l, 0), lambda: half(r, 1))[k]()
            return remote(ref, ref, send.at[k], recv.at[k], ring.device((r, l, r, l)[k]))

        self.copies = Copies(make, 4)

    def start(self):
        self.copies[0].start()
        self.copies[1].start()

    def middle(self):
        self.copies[0].wait_recv()
        self.copies[2].start()
        self.copies[1].wait_recv()
        self.copies[3].start()

    def arrived(self):
        self.copies[2].wait_recv()
        self.copies[3].wait_recv()

    def sent(self):
        for copy in self.copies:
            copy.wait_send()


def grouped(ref, order, i, low, count):
    if order == 0:
        return ref.at[i, pl.ds(low, count)]
    return ref.at[pl.ds(low, count), i]


def block_of(ref, order, i, j):
    return ref.at[i, j] if order == 0 else ref.at[j, i]


def kernel(
    ctx_in, res_in, gain_in, w_out_in, w_up_hbm, w_down_hbm, ups_in,
    res_out, ctx_out, gain_out, w_out_out, w_up_out, w_down_out,
    w_up, w_down, part, land1, land2, act_grad, pre_grad, act,
    ctx_all, ctx_part, ctx_land1, ctx_land2, ups_all, normed_all, res_all, normed_t, total,
    z_part, z_sib, z_land, stat_x, stat_y, unit, inv, gain_sib, gain_z, up_stage, down_stage, act_t,
    w_sem, s1, v1, s2, v2, gs, gv, asend, arecv, cs, cv, c1s, c1v, c2s, c2v,
    zgs, zgv, zss, zsv, sts, stv, ggs, ggv, out_sem,
):
    row, col = lax.axis_index("row"), lax.axis_index("col")
    z, core = row // 2, lax.rem(row, 2)
    x, y = col // 4, lax.rem(col, 4)
    ring_x = Ring(x, lambda i: {"col": i * 4 + y})
    ring_y = Ring(y, lambda i: {"col": x * 4 + i})
    ring_z = Ring(z, lambda i: {"row": i * 2 + core})
    sibling = {"row": z * 2 + 1 - core}
    rings = (ring_x, ring_y)

    load_down = pltpu.make_async_copy(w_down_hbm, w_down, w_sem.at[0])
    load_up = pltpu.make_async_copy(w_up_hbm, w_up, w_sem.at[1])
    load_down.start()
    load_up.start()

    barrier = pltpu.get_barrier_semaphore()
    for ring in (ring_x, ring_y, ring_z):
        for i in (ring.left, ring.right, ring.opposite):
            pl.semaphore_signal(barrier, inc=1, device_id=ring.device(i), device_id_type=MESH)
    pl.semaphore_signal(barrier, inc=1, device_id=sibling, device_id_type=MESH)
    pl.semaphore_wait(barrier, 10)

    def scatter1(ref, landing, send, recv, order):
        ring = rings[order]
        return Scatter(ring, lambda i, h: grouped(ref, order, i, 2 * h, 2), landing, send, recv)

    def scatter2(ref, landing, send, recv, order, rows):
        mine, ring = rings[order].place, rings[1 - order]
        return Scatter(
            ring,
            lambda j, h: block_of(ref, order, mine, j).at[pl.ds(h * rows, rows)],
            landing, send, recv,
        )

    def gather1(ref, send, recv, order):
        mine, ring = rings[order].place, rings[1 - order]
        return Gather(
            ring,
            lambda j: block_of(ref, order, mine, j),
            lambda j, h: block_of(ref, order, mine, j).at[pl.ds(h * 32, 32)],
            send.at[pl.ds(0, 4)], recv.at[pl.ds(0, 4)],
        )

    def gather2(ref, send, recv, order):
        return Gather(
            rings[order],
            lambda i: grouped(ref, order, i, 0, 4),
            lambda i, h: grouped(ref, order, i, 2 * h, 2),
            send.at[pl.ds(4, 4)], recv.at[pl.ds(4, 4)],
        )

    def scatter_turn(ref, landing, send, recv, order):
        one = scatter1(ref, landing, send, recv, order)
        first, second = one.finish()
        one.half(one.ring.place, 0)[...] = first.astype(BF16)
        one.half(one.ring.place, 1)[...] = second.astype(BF16)

    class RowGather:
        def __init__(self, ref, n):
            self.ring = Gather(
                ring_z,
                lambda i: ref.at[i, core],
                lambda i, h: ref.at[i, core, pl.ds(h * 64, 64)],
                zgs.at[n, pl.ds(0, 4)], zgv.at[n, pl.ds(0, 4)],
            )
            blocks = (z, ring_z.left, ring_z.right, ring_z.opposite)
            self.near = Copies(
                lambda k: remote(
                    ref.at[blocks[k], core], ref.at[blocks[k], core],
                    zgs.at[n, 4 + k], zgv.at[n, 4 + k], sibling,
                ),
                4,
            )

        def start(self):
            self.ring.start()
            self.near[0].start()

        def middle(self):
            self.ring.middle()
            self.near[1].start()
            self.near[2].start()

        def last(self):
            self.ring.arrived()
            self.near[3].start()

        def finish(self):
            for copy in self.near:
                copy.wait_recv()
            for copy in self.near:
                copy.wait_send()
            self.ring.sent()

    def row_near():
        return remote(z_part.at[:, 1 - core], z_sib, zss.at[6], zsv.at[6], sibling)

    row_ring = Scatter(
        ring_z, lambda i, h: z_part.at[i, core, pl.ds(h * 64, 64)], z_land, zss, zsv
    )

    def row_scatter_ring():
        row_near().wait_recv()
        row_near().wait_send()
        z_part[:, core] = (z_part[:, core].astype(F32) + z_sib[...].astype(F32)).astype(BF16)
        row_ring.start()

    def stat_copies(n, ref, ring):
        base = 0 if ref is stat_x else 3
        return Copies(
            lambda d: remote(
                ref.at[n, ring.place], ref.at[n, ring.place],
                sts.at[n, base + d], stv.at[n, base + d],
                ring.device(lax.rem(ring.place + 1 + d, 4)),
            ),
            3,
        )

    def to_lanes(first, second):
        lane = lax.broadcasted_iota(jnp.int32, (128, 128), 1)
        both = jnp.where(lane == 0, first, jnp.where(lane == 1, second, 0.0))
        return jnp.transpose(both)[0:8]

    def to_rows(values):
        return jnp.transpose(jnp.broadcast_to(values, (128, 128)))[:, 0:1]

    def stat_start(n, ref, ring, values):
        ref[n, ring.place] = values
        for copy in stat_copies(n, ref, ring):
            copy.start()

    def stat_wait(n, ref, ring):
        for copy in stat_copies(n, ref, ring):
            copy.wait_recv()
        for copy in stat_copies(n, ref, ring):
            copy.wait_send()

    def merge_moments(ref, count):
        means = [ref[0, i, 0:1] for i in range(4)]
        mean = (means[0] + means[1] + means[2] + means[3]) * 0.25
        squares = ref[0, 0, 1:2] + ref[0, 1, 1:2] + ref[0, 2, 1:2] + ref[0, 3, 1:2]
        for one in means:
            squares += count * (one - mean) * (one - mean)
        return mean, squares

    def two_rows(first, second):
        line = lax.broadcasted_iota(jnp.int32, (8, 128), 0)
        return jnp.where(line == 0, first, jnp.where(line == 1, second, 0.0))

    ups_gather, normed_gather, res_gather = (
        RowGather(ref, n) for n, ref in enumerate((ups_all, normed_all, res_all))
    )

    def project_out():
        @pl.loop(0, 4)
        def _(m):
            value = dot(ctx_all[0, m].reshape(256, CH), w_out_in[0:CH, :]) + dot(
                ctx_all[1, m].reshape(256, CH), w_out_in[CH:W, :]
            )
            z_part[m] = value.astype(BF16).reshape(2, 128, W)

        row_near().start()

    def row_moments():
        first, second = row_ring.finish()
        for h, share in enumerate((first, second)):
            unit[pl.ds(h * 64, 64)] = share + res_in[pl.ds(h * 64, 64)].astype(F32)
        summed = unit[...]
        mean = jnp.sum(summed, axis=1, keepdims=True) * (1.0 / W)
        centered = summed - mean
        squares = jnp.sum(centered * centered, axis=1, keepdims=True)
        stat_start(0, stat_x, ring_x, to_lanes(mean, squares))

    def moments_x():
        stat_wait(0, stat_x, ring_x)
        stat_start(0, stat_y, ring_y, two_rows(*merge_moments(stat_x, float(W))))

    def normalize():
        stat_wait(0, stat_y, ring_y)
        mean, squares = merge_moments(stat_y, float(4 * W))
        inv_row = lax.rsqrt(squares * (1.0 / D) + 1e-05)
        inv_std = to_rows(inv_row)
        inv[...] = jnp.broadcast_to(inv_std, (128, 128))
        rows = (unit[...] - to_rows(mean)) * inv_std
        unit[...] = rows
        normed_all[z, core] = (rows * gain_in[...]).astype(BF16)
        normed_gather.start()

    def normed_done():
        normed_gather.finish()
        load_up.wait()

        @pl.loop(0, 4)
        def _(m):
            for c in range(2):
                tokens = pl.ds(pl.multiple_of((m * 2 + c) * 128, 128), 128)
                normed_t[:, tokens] = jnp.transpose(normed_all[m, c])

    def unit_scatter1(i, order):
        slot = lax.rem(i, PAIRS)
        return (
            part.at[slot, order], land1.at[slot, order], s1.at[slot, order], v1.at[slot, order], order
        )

    def unit_scatter2(i, order):
        slot = lax.rem(i, PAIRS)
        return (
            part.at[slot, order], land2.at[slot, order], s2.at[slot, order], v2.at[slot, order], order, 32
        )

    def columns(p, order):
        return pl.ds(pl.multiple_of((p * 2 + order) * C, C), C)

    def multiply(i):
        slot = lax.rem(i, PAIRS)

        @pl.when(i < PAIRS)
        def _():
            for order in range(2):

                @pl.loop(0, 4)
                def _(m):
                    value = dot_cols(ups_all[m].reshape(256, W), w_down[columns(i, order), :])
                    part[slot, order, m] = value.astype(BF16).reshape(4, 64, C)

                scatter1(*unit_scatter1(i, order)).start()

        @pl.when(i >= PAIRS)
        def _():
            for order in range(2):

                @pl.loop(0, 4)
                def _(m):
                    value = dot(normed_all[m].reshape(256, W), w_up[:, columns(i - PAIRS, order)])
                    part[slot, order, m] = value.astype(BF16).reshape(4, 64, C)

                scatter1(*unit_scatter1(i, order)).start()

    def scatter1_middle(i):
        for order in range(2):
            scatter1(*unit_scatter1(i, order)).middle()

    def scatter1_finish(i):
        for order in range(2):
            scatter_turn(*unit_scatter1(i, order))
            scatter2(*unit_scatter2(i, order)).start()

    def scatter2_middle(i):
        for order in range(2):
            scatter2(*unit_scatter2(i, order)).middle()

    def pre_gather(p, order, stage):
        return (gather1, gather2)[stage](
            pre_grad.at[p, order], gs.at[p, order], gv.at[p, order], order
        )

    def act_gather(p, order, stage):
        return (gather1, gather2)[stage](
            act.at[p, order], asend.at[p, order], arecv.at[p, order], order
        )

    def scatter2_finish(i):
        slot = lax.rem(i, PAIRS)
        for order in range(2):
            halves = scatter2(*unit_scatter2(i, order)).finish()

            @pl.when(i < PAIRS)
            def _():
                for h in range(2):
                    act_grad[slot, order, pl.ds(h * 32, 32)] = halves[h]

            @pl.when(i >= PAIRS)
            def _():
                for h in range(2):
                    value, slope = gelu_parts(halves[h])
                    grad = act_grad[slot, order, pl.ds(h * 32, 32)] * slope
                    act[slot, order, x, y, pl.ds(h * 32, 32)] = value.astype(BF16)
                    pre_grad[slot, order, x, y, pl.ds(h * 32, 32)] = grad.astype(BF16)
                pre_gather(slot, order, 0).start()

    def gather_steps(make):
        def start(p):
            for order in range(2):
                make(p, order, 0).start()

        def middle1(p):
            for order in range(2):
                make(p, order, 0).middle()

        def turn(p):
            for order in range(2):
                one = make(p, order, 0)
                one.arrived()
                one.sent()
                make(p, order, 1).start()

        def middle2(p):
            for order in range(2):
                make(p, order, 1).middle()

        def finish(p):
            for order in range(2):
                one = make(p, order, 1)
                one.arrived()
                one.sent()

        return start, middle1, turn, middle2, finish

    _, pre_middle1, pre_turn, pre_middle2, pre_finish = gather_steps(pre_gather)
    act_start, act_middle1, act_turn, act_middle2, act_finish = gather_steps(act_gather)

    def up_store(p, order):
        slot = lax.rem(p, 2)
        return pltpu.make_async_copy(
            up_stage.at[slot, order], w_up_out.at[:, columns(p, order)], out_sem.at[0, slot, order]
        )

    def down_store(p, order):
        slot = lax.rem(p, 2)
        return pltpu.make_async_copy(
            down_stage.at[slot, order], w_down_out.at[columns(p, order), :], out_sem.at[1, slot, order]
        )

    def pre_products(p):
        slot = lax.rem(p, 2)
        for order in range(2):

            @pl.when(p >= 2)
            def _():
                up_store(p - 2, order).wait()

            @pl.loop(0, 3)
            def _(n):
                rows = pl.ds(pl.multiple_of(n * 256, 256), 256)
                value = dot(normed_t[rows, :], pre_grad[p, order].reshape(1024, C))
                up_stage[slot, order, rows, :] = value.astype(BF16)

            up_store(p, order).start()

        @pl.loop(0, 4)
        def _(m):
            value = dot_cols(pre_grad[p, 0, m].reshape(256, C), w_up[:, columns(p, 0)]) + dot_cols(
                pre_grad[p, 1, m].reshape(256, C), w_up[:, columns(p, 1)]
            )
            value = value.reshape(2, 128, W)

            @pl.when(p == 0)
            def _():
                total[m] = value

            @pl.when(p > 0)
            def _():
                total[m] += value

    def act_products(p):
        slot = lax.rem(p, 2)
        for order in range(2):

            @pl.when(p >= 2)
            def _():
                down_store(p - 2, order).wait()

            for m in range(4):
                act_t[:, pl.ds(m * 256, 256)] = jnp.transpose(act[p, order, m].reshape(256, C))

            @pl.loop(0, 3)
            def _(n):
                cols = pl.ds(pl.multiple_of(n * 256, 256), 256)
                value = dot(act_t[...], ups_all[:, :, :, cols].reshape(1024, 256))
                down_stage[slot, order, :, cols] = value.astype(BF16)

            down_store(p, order).start()

    def reduce_rows():
        z_part[...] = total[...].astype(BF16)
        row_near().start()

    def gain_near():
        return remote(gain_sib.at[0], gain_sib.at[1], ggs.at[0], ggv.at[0], sibling)

    gain_far = Copies(
        lambda d: remote(
            gain_z.at[z], gain_z.at[z], ggs.at[1 + d], ggv.at[1 + d],
            ring_z.device(lax.rem(z + 1 + d, 4)),
        ),
        3,
    )

    def grad_sums():
        first, second = row_ring.finish()
        for h, share in enumerate((first, second)):
            total[0, 0, pl.ds(h * 64, 64)] = share
        grad = total[0, 0]
        aligned = grad * unit[...]
        scaled = grad * gain_in[...]
        stat_start(
            1, stat_x, ring_x,
            to_lanes(
                jnp.sum(scaled, axis=1, keepdims=True),
                jnp.sum(scaled * unit[...], axis=1, keepdims=True),
            ),
        )
        gain_sib[0] = jnp.broadcast_to(jnp.sum(aligned, axis=0, keepdims=True), (8, W))
        gain_near().start()

    def sums_x():
        stat_wait(1, stat_x, ring_x)
        stat_start(
            1, stat_y, ring_y, stat_x[1, 0] + stat_x[1, 1] + stat_x[1, 2] + stat_x[1, 3]
        )
        gain_near().wait_recv()
        gain_near().wait_send()
        gain_z[z] = gain_sib[0] + gain_sib[1]
        for copy in gain_far:
            copy.start()

    def grad_rows():
        stat_wait(1, stat_y, ring_y)
        means = (stat_y[1, 0] + stat_y[1, 1] + stat_y[1, 2] + stat_y[1, 3]) * (1.0 / D)
        scaled = total[0, 0] * gain_in[...]
        value = ups_in[...].astype(F32) + inv[:, 0:1] * (
            scaled - to_rows(means[0:1]) - unit[...] * to_rows(means[1:2])
        )
        rounded = value.astype(BF16)
        res_out[...] = rounded
        res_all[z, core] = rounded
        res_gather.start()

    def gain_done():
        for copy in gain_far:
            copy.wait_recv()
        for copy in gain_far:
            copy.wait_send()
        gain_out[...] = gain_z[0] + gain_z[1] + gain_z[2] + gain_z[3]

    def ctx_scatter1(order):
        return ctx_part.at[order], ctx_land1.at[order], c1s.at[order], c1v.at[order], order

    def ctx_scatter2(order):
        return ctx_part.at[order], ctx_land2.at[order], c2s.at[order], c2v.at[order], order, 32

    def context_product():
        res_gather.finish()
        for order in range(2):

            @pl.loop(0, 4)
            def _(m):
                value = dot_cols(
                    res_all[m].reshape(256, W), w_out_in[pl.ds(order * CH, CH), :]
                )
                ctx_part[order, m] = value.astype(BF16).reshape(4, 64, CH)

            scatter1(*ctx_scatter1(order)).start()

    def context_middle1():
        for order in range(2):
            scatter1(*ctx_scatter1(order)).middle()

    def context_turn():
        for order in range(2):
            scatter_turn(*ctx_scatter1(order))
            scatter2(*ctx_scatter2(order)).start()

    def context_middle2():
        for order in range(2):
            scatter2(*ctx_scatter2(order)).middle()

    def context_finish():
        for order in range(2):
            for h, share in enumerate(scatter2(*ctx_scatter2(order)).finish()):
                ctx_out[pl.ds(h * 32, 32), pl.ds(order * CH, CH)] = share.astype(BF16)

    def out_product():
        for order in range(2):
            for n in range(3):
                cols = pl.ds(n * 256, 256)
                value = lax.dot_general(
                    ctx_all[order].reshape(1024, CH),
                    res_all[:, :, :, cols].reshape(1024, 256),
                    (((0,), (0,)), ((), ())),
                    preferred_element_type=F32,
                )
                w_out_out[pl.ds(order * CH, CH), cols] = value.astype(BF16)

    ups_all[z, core] = ups_in[...]
    ups_gather.start()
    for order in range(2):
        ctx_all[order, x, y] = ctx_in[:, pl.ds(order * CH, CH)]
        gather1(ctx_all.at[order], cs.at[order], cv.at[order], order).start()
    for order in range(2):
        gather1(ctx_all.at[order], cs.at[order], cv.at[order], order).middle()
    ups_gather.middle()
    for order in range(2):
        one = gather1(ctx_all.at[order], cs.at[order], cv.at[order], order)
        one.arrived()
        one.sent()
        gather2(ctx_all.at[order], cs.at[order], cv.at[order], order).start()
    ups_gather.last()
    for order in range(2):
        gather2(ctx_all.at[order], cs.at[order], cv.at[order], order).middle()
    ups_gather.finish()
    load_down.wait()

    def context_arrived():
        for order in range(2):
            one = gather2(ctx_all.at[order], cs.at[order], cv.at[order], order)
            one.arrived()
            one.sent()
        project_out()

    early = {
        1: [row_scatter_ring],
        2: [row_moments],
        3: [normalize],
        4: [normed_gather.middle],
        5: [normed_gather.last],
        6: [normed_done],
        20: [row_scatter_ring],
        21: [grad_sums],
        22: [grad_rows],
        23: [res_gather.last],
        24: [context_middle1],
        25: [context_turn],
        26: [context_middle2],
        27: [context_finish],
    }
    late = {
        0: [context_arrived],
        1: [row_ring.middle],
        2: [moments_x],
        19: [reduce_rows],
        20: [row_ring.middle],
        21: [sums_x],
        22: [gain_done, res_gather.middle],
        23: [context_product],
        24: [out_product],
    }
    base = PAIRS + 4
    act_base = base + ACT_DELAY
    steps = [
        (act_base + 4, PAIRS, act_finish),
        (act_base + 3, PAIRS, act_middle2),
        (act_base + 2, PAIRS, act_turn),
        (act_base + 1, PAIRS, act_middle1),
        (base + 4, PAIRS, pre_finish),
        (base + 3, PAIRS, pre_middle2),
        (base + 2, PAIRS, pre_turn),
        (base + 1, PAIRS, pre_middle1),
        (4, 2 * PAIRS, scatter2_finish),
        (3, 2 * PAIRS, scatter2_middle),
        (2, 2 * PAIRS, scatter1_finish),
        (1, 2 * PAIRS, scatter1_middle),
        (0, 2 * PAIRS, multiply),
        (act_base, PAIRS, act_start),
        (base + 4, PAIRS, pre_products),
        (act_base + 4, PAIRS, act_products),
    ]

    def at_ticks(tick, events):
        for when, calls in events.items():

            @pl.when(tick == when)
            def _(calls=calls):
                for call in calls:
                    call()

    @pl.loop(0, TICKS)
    def _(tick):
        at_ticks(tick, early)
        for first, count, step in steps:

            @pl.when((tick >= first) & (tick < first + count))
            def _(first=first, step=step):
                step(tick - first)

        at_ticks(tick, late)

    for p in (PAIRS - 2, PAIRS - 1):
        for order in range(2):
            up_store(p, order).wait()
            down_store(p, order).wait()


def on_device(context, residual, norm_gain, w_out, w_up, w_down, upstream):
    vmem = pl.BlockSpec(memory_space=pltpu.VMEM)
    hbm = pl.BlockSpec(memory_space=pl.ANY)
    shape = jax.ShapeDtypeStruct
    dma = pltpu.SemaphoreType.DMA
    outs = pl.pallas_call(
        kernel,
        out_shape=(
            shape((128, W), BF16),
            shape((64, W), BF16),
            shape((8, W), F32),
            shape((W, W), BF16),
            shape((W, 3072), BF16),
            shape((3072, W), BF16),
        ),
        in_specs=[vmem, vmem, vmem, vmem, hbm, hbm, vmem],
        out_specs=(vmem, vmem, vmem, vmem, hbm, hbm),
        scratch_shapes=[
            pltpu.VMEM((W, 3072), BF16),
            pltpu.VMEM((3072, W), BF16),
            pltpu.VMEM((PAIRS, 2, 4, 4, 64, C), BF16),
            pltpu.VMEM((PAIRS, 2, 6, 2, 64, C), BF16),
            pltpu.VMEM((PAIRS, 2, 6, 32, C), BF16),
            pltpu.VMEM((PAIRS, 2, 64, C), F32),
            pltpu.VMEM((PAIRS, 2, 4, 4, 64, C), BF16),
            pltpu.VMEM((PAIRS, 2, 4, 4, 64, C), BF16),
            pltpu.VMEM((2, 4, 4, 64, CH), BF16),
            pltpu.VMEM((2, 4, 4, 64, CH), BF16),
            pltpu.VMEM((2, 6, 2, 64, CH), BF16),
            pltpu.VMEM((2, 6, 32, CH), BF16),
            pltpu.VMEM((4, 2, 128, W), BF16),
            pltpu.VMEM((4, 2, 128, W), BF16),
            pltpu.VMEM((4, 2, 128, W), BF16),
            pltpu.VMEM((W, 1024), BF16),
            pltpu.VMEM((4, 2, 128, W), F32),
            pltpu.VMEM((4, 2, 128, W), BF16),
            pltpu.VMEM((4, 128, W), BF16),
            pltpu.VMEM((6, 64, W), BF16),
            pltpu.VMEM((2, 4, 8, 128), F32),
            pltpu.VMEM((2, 4, 8, 128), F32),
            pltpu.VMEM((128, W), F32),
            pltpu.VMEM((128, 128), F32),
            pltpu.VMEM((2, 8, W), F32),
            pltpu.VMEM((4, 8, W), F32),
            pltpu.VMEM((2, 2, W, C), BF16),
            pltpu.VMEM((2, 2, C, W), BF16),
            pltpu.VMEM((C, 1024), BF16),
            dma((2,)),
            dma((PAIRS, 2, 6)),
            dma((PAIRS, 2, 6)),
            dma((PAIRS, 2, 6)),
            dma((PAIRS, 2, 6)),
            dma((PAIRS, 2, 8)),
            dma((PAIRS, 2, 8)),
            dma((PAIRS, 2, 8)),
            dma((PAIRS, 2, 8)),
            dma((2, 8)),
            dma((2, 8)),
            dma((2, 6)),
            dma((2, 6)),
            dma((2, 6)),
            dma((2, 6)),
            dma((3, 8)),
            dma((3, 8)),
            dma((7,)),
            dma((7,)),
            dma((2, 6)),
            dma((2, 6)),
            dma((4,)),
            dma((4,)),
            dma((2, 2, 2)),
        ],
        compiler_params=pltpu.CompilerParams(
            collective_id=0, has_side_effects=True, vmem_limit_bytes=63 * 1024 * 1024
        ),
        cost_estimate=pl.CostEstimate(
            flops=28_000_000_000, bytes_accessed=25_000_000, transcendentals=200_000
        ),
    )(context, residual, norm_gain.reshape(1, W), w_out, w_up, w_down, upstream)
    return outs[0], outs[1], outs[2][0], outs[3], outs[4], outs[5]


def solution(mesh):
    return jax.shard_map(
        on_device,
        mesh=mesh,
        in_specs=(
            P("col", "row"),
            P("row", "col"),
            P("col"),
            P("row", "col"),
            P("col", "row"),
            P("row", "col"),
            P("row", "col"),
        ),
        out_specs=(
            P("row", "col"),
            P("col", "row"),
            P("col"),
            P("row", "col"),
            P("col", "row"),
            P("row", "col"),
        ),
        check_vma=False,
    )
```

```python
import jax
import jax.numpy as jnp
from jax import lax
from jax.experimental import pallas as pl
from jax.experimental.pallas import tpu as pltpu
from jax.sharding import PartitionSpec as P

MESH = pl.DeviceIdType.MESH
BF16 = jnp.bfloat16
F32 = jnp.float32
D = 12288
W = 768
PAIRS = 6
C = 256
CH = 384
ACT_DELAY = 6
TICKS = 28
CUTS = 4


def gelu_parts(values):
    tanh_val = jnp.tanh(0.7978845608028654 * (values + 0.044715 * values * values * values))
    value = 0.5 * values * (1.0 + tanh_val)
    slope = 0.5 * (1.0 + tanh_val) + 0.5 * values * (
        1.0 - tanh_val * tanh_val
    ) * 0.7978845608028654 * (1.0 + 0.134145 * values * values)
    return value, slope


def dot(first_op, second_op):
    return jnp.dot(first_op, second_op, preferred_element_type=F32)


def dot_cols(first_op, second_op):
    return lax.dot_general(
        first_op, second_op, (((1,), (1,)), ((), ())), preferred_element_type=F32
    )


class Ring:
    def __init__(self, place, device):
        self.place = place
        self.right = lax.rem(place + 1, 4)
        self.opposite = lax.rem(place + 2, 4)
        self.left = lax.rem(place + 3, 4)
        self.device = device


def remote(src, dst, send, recv, device):
    return pltpu.make_async_remote_copy(
        src_ref=src, dst_ref=dst, send_sem=send, recv_sem=recv, device_id=device, device_id_type=MESH
    )


class Copies:
    def __init__(self, make, count):
        self.make, self.count = make, count

    def __getitem__(self, k):
        return self.make(k)

    def __iter__(self):
        return (self.make(k) for k in range(self.count))


class Scatter:
    def __init__(self, ring, half, landing, send, recv):
        r, l, o = ring.right, ring.left, ring.opposite
        plan = [(o, 0, r), (r, 1, r), (r, 0, r), (o, 1, l), (l, 0, l), (l, 1, l)]
        self.ring, self.half, self.landing = ring, half, landing

        def make(k):
            i, h, to = plan[k]
            return remote(half(i, h), landing.at[k], send.at[k], recv.at[k], ring.device(to))

        self.copies = Copies(make, 6)

    def start(self):
        for k in (0, 3, 1, 4):
            self.copies[k].start()

    def middle(self):
        for k, i, h, nxt in ((0, self.ring.right, 0, 2), (3, self.ring.left, 1, 5)):
            self.copies[k].wait_recv()
            part = self.half(i, h)
            part[...] = (part[...].astype(F32) + self.landing[k].astype(F32)).astype(BF16)
            self.copies[nxt].start()

    def finish(self):
        for k in (1, 4, 2, 5):
            self.copies[k].wait_recv()
        for copy in self.copies:
            copy.wait_send()
        me = self.ring.place
        first = (
            self.half(me, 0)[...].astype(F32)
            + self.landing[2].astype(F32)
            + self.landing[4].astype(F32)
        )
        second = (
            self.half(me, 1)[...].astype(F32)
            + self.landing[1].astype(F32)
            + self.landing[5].astype(F32)
        )
        return first, second


class Gather:
    def __init__(self, ring, group, half, send, recv):
        r, l = ring.right, ring.left
        me = ring.place

        def make(k):
            ref = (lambda: group(me), lambda: group(me), lambda: half(l, 0), lambda: half(r, 1))[k]()
            return remote(ref, ref, send.at[k], recv.at[k], ring.device((r, l, r, l)[k]))

        self.copies = Copies(make, 4)

    def start(self):
        self.copies[0].start()
        self.copies[1].start()

    def middle(self):
        self.copies[0].wait_recv()
        self.copies[2].start()
        self.copies[1].wait_recv()
        self.copies[3].start()

    def arrived(self):
        self.copies[2].wait_recv()
        self.copies[3].wait_recv()

    def sent(self):
        for copy in self.copies:
            copy.wait_send()


class HalfGather:
    def __init__(self, ring, half, send, recv):
        r, l, me = ring.right, ring.left, ring.place
        plan = [(me, 0, r), (me, 1, r), (me, 1, l), (me, 0, l), (l, 0, r), (r, 1, l)]

        def make(k):
            i, h, to = plan[k]
            return remote(half(i, h), half(i, h), send.at[k], recv.at[k], ring.device(to))

        self.copies = Copies(make, 6)

    def start(self):
        for k in (0, 2, 1, 3):
            self.copies[k].start()

    def middle(self):
        for first, forward in ((0, 4), (2, 5)):
            self.copies[first].wait_recv()
            self.copies[forward].start()
        for rest in (1, 3):
            self.copies[rest].wait_recv()

    def arrived(self):
        self.copies[4].wait_recv()
        self.copies[5].wait_recv()

    def sent(self):
        for copy in self.copies:
            copy.wait_send()


def grouped(ref, order, i, low, count):
    if order == 0:
        return ref.at[i, pl.ds(low, count)]
    return ref.at[pl.ds(low, count), i]


def block_of(ref, order, i, j):
    return ref.at[i, j] if order == 0 else ref.at[j, i]


def kernel(
    ctx_in, res_in, gain_in, w_out_in, w_up_hbm, w_down_hbm, ups_in,
    res_out, ctx_out, gain_out, w_out_out, w_up_out, w_down_out,
    w_up, w_down, part, land1, land2, act_grad, pre_grad, act,
    ctx_all, ctx_part, ctx_land1, ctx_land2, ups_all, normed_all, res_all, normed_t, total,
    z_part, z_sib, z_land, stat_x, stat_y, unit, inv, gain_sib, gain_z, up_stage, down_stage, act_t,
    w_sem, s1, v1, s2, v2, gs, gv, asend, arecv, cs, cv, c1s, c1v, c2s, c2v,
    zgs, zgv, zss, zsv, sts, stv, ggs, ggv, out_sem,
):
    row, col = lax.axis_index("row"), lax.axis_index("col")
    z, core = row // 2, lax.rem(row, 2)
    x, y = col // 4, lax.rem(col, 4)
    ring_x = Ring(x, lambda i: {"col": i * 4 + y})
    ring_y = Ring(y, lambda i: {"col": x * 4 + i})
    ring_z = Ring(z, lambda i: {"row": i * 2 + core})
    sibling = {"row": z * 2 + 1 - core}
    rings = (ring_x, ring_y)

    load_down = pltpu.make_async_copy(w_down_hbm, w_down, w_sem.at[0])
    load_up = pltpu.make_async_copy(w_up_hbm, w_up, w_sem.at[1])
    load_down.start()
    load_up.start()

    barrier = pltpu.get_barrier_semaphore()
    for ring in (ring_x, ring_y, ring_z):
        for i in (ring.left, ring.right, ring.opposite):
            pl.semaphore_signal(barrier, inc=1, device_id=ring.device(i), device_id_type=MESH)
    pl.semaphore_signal(barrier, inc=1, device_id=sibling, device_id_type=MESH)
    pl.semaphore_wait(barrier, 10)

    def scatter1(ref, landing, send, recv, order):
        ring = rings[order]
        return Scatter(ring, lambda i, h: grouped(ref, order, i, 2 * h, 2), landing, send, recv)

    def scatter2(ref, landing, send, recv, order, rows):
        mine, ring = rings[order].place, rings[1 - order]
        return Scatter(
            ring,
            lambda j, h: block_of(ref, order, mine, j).at[pl.ds(h * rows, rows)],
            landing, send, recv,
        )

    def gather1(ref, send, recv, order):
        mine, ring = rings[order].place, rings[1 - order]
        return Gather(
            ring,
            lambda j: block_of(ref, order, mine, j),
            lambda j, h: block_of(ref, order, mine, j).at[pl.ds(h * 32, 32)],
            send.at[pl.ds(0, 4)], recv.at[pl.ds(0, 4)],
        )

    def gather2(ref, send, recv, order):
        return Gather(
            rings[order],
            lambda i: grouped(ref, order, i, 0, 4),
            lambda i, h: grouped(ref, order, i, 2 * h, 2),
            send.at[pl.ds(4, 4)], recv.at[pl.ds(4, 4)],
        )

    def context_gather1(order):
        ref, mine = ctx_all.at[order], rings[order].place
        return HalfGather(
            rings[1 - order],
            lambda j, h: block_of(ref, order, mine, j).at[pl.ds(h * 32, 32)],
            cs.at[order, pl.ds(0, 6)], cv.at[order, pl.ds(0, 6)],
        )

    def context_gather2(order):
        return HalfGather(
            rings[order],
            lambda i, h: grouped(ctx_all.at[order], order, i, 2 * h, 2),
            cs.at[order, pl.ds(6, 6)], cv.at[order, pl.ds(6, 6)],
        )

    def scatter_turn(ref, landing, send, recv, order):
        one = scatter1(ref, landing, send, recv, order)
        first, second = one.finish()
        one.half(one.ring.place, 0)[...] = first.astype(BF16)
        one.half(one.ring.place, 1)[...] = second.astype(BF16)

    class RowGather:
        def __init__(self, ref, n):
            self.ring = HalfGather(
                ring_z,
                lambda i, h: ref.at[i, core, pl.ds(h * 64, 64)],
                zgs.at[n, pl.ds(0, 6)], zgv.at[n, pl.ds(0, 6)],
            )
            blocks = (z, ring_z.left, ring_z.right, ring_z.opposite)
            self.near = Copies(
                lambda k: remote(
                    ref.at[blocks[k], core], ref.at[blocks[k], core],
                    zgs.at[n, 6 + k], zgv.at[n, 6 + k], sibling,
                ),
                4,
            )

        def start(self):
            self.ring.start()
            self.near[0].start()

        def middle(self):
            self.ring.middle()
            self.near[1].start()
            self.near[2].start()

        def last(self):
            self.ring.arrived()
            self.near[3].start()

        def finish(self):
            for copy in self.near:
                copy.wait_recv()
            for copy in self.near:
                copy.wait_send()
            self.ring.sent()

    def row_near():
        return remote(z_part.at[:, 1 - core], z_sib, zss.at[6], zsv.at[6], sibling)

    row_ring = Scatter(
        ring_z, lambda i, h: z_part.at[i, core, pl.ds(h * 64, 64)], z_land, zss, zsv
    )

    def row_scatter_ring():
        row_near().wait_recv()
        row_near().wait_send()
        z_part[:, core] = (z_part[:, core].astype(F32) + z_sib[...].astype(F32)).astype(BF16)
        row_ring.start()

    def stat_copies(n, ref, ring):
        base = 0 if ref is stat_x else 3
        return Copies(
            lambda d: remote(
                ref.at[n, ring.place], ref.at[n, ring.place],
                sts.at[n, base + d], stv.at[n, base + d],
                ring.device(lax.rem(ring.place + 1 + d, 4)),
            ),
            3,
        )

    def to_lanes(first, second):
        lane = lax.broadcasted_iota(jnp.int32, (128, 128), 1)
        both = jnp.where(lane == 0, first, jnp.where(lane == 1, second, 0.0))
        return jnp.transpose(both)[0:8]

    def to_rows(values):
        return jnp.transpose(jnp.broadcast_to(values, (128, 128)))[:, 0:1]

    def stat_start(n, ref, ring, values):
        ref[n, ring.place] = values
        for copy in stat_copies(n, ref, ring):
            copy.start()

    def stat_wait(n, ref, ring):
        for copy in stat_copies(n, ref, ring):
            copy.wait_recv()
        for copy in stat_copies(n, ref, ring):
            copy.wait_send()

    def merge_moments(ref, count):
        means = [ref[0, i, 0:1] for i in range(4)]
        mean = (means[0] + means[1] + means[2] + means[3]) * 0.25
        squares = ref[0, 0, 1:2] + ref[0, 1, 1:2] + ref[0, 2, 1:2] + ref[0, 3, 1:2]
        for one in means:
            squares += count * (one - mean) * (one - mean)
        return mean, squares

    def two_rows(first, second):
        line = lax.broadcasted_iota(jnp.int32, (8, 128), 0)
        return jnp.where(line == 0, first, jnp.where(line == 1, second, 0.0))

    ups_gather, normed_gather, res_gather = (
        RowGather(ref, n) for n, ref in enumerate((ups_all, normed_all, res_all))
    )

    def project_out():
        @pl.loop(0, 4)
        def _(m):
            value = dot(ctx_all[0, m].reshape(256, CH), w_out_in[0:CH, :]) + dot(
                ctx_all[1, m].reshape(256, CH), w_out_in[CH:W, :]
            )
            z_part[m] = value.astype(BF16).reshape(2, 128, W)

        row_near().start()

    def row_moments():
        first, second = row_ring.finish()
        for h, share in enumerate((first, second)):
            unit[pl.ds(h * 64, 64)] = share + res_in[pl.ds(h * 64, 64)].astype(F32)
        summed = unit[...]
        mean = jnp.sum(summed, axis=1, keepdims=True) * (1.0 / W)
        centered = summed - mean
        squares = jnp.sum(centered * centered, axis=1, keepdims=True)
        stat_start(0, stat_x, ring_x, to_lanes(mean, squares))

    def moments_x():
        stat_wait(0, stat_x, ring_x)
        stat_start(0, stat_y, ring_y, two_rows(*merge_moments(stat_x, float(W))))

    def normalize():
        stat_wait(0, stat_y, ring_y)
        mean, squares = merge_moments(stat_y, float(4 * W))
        inv_row = lax.rsqrt(squares * (1.0 / D) + 1e-05)
        inv_std = to_rows(inv_row)
        inv[...] = jnp.broadcast_to(inv_std, (128, 128))
        rows = (unit[...] - to_rows(mean)) * inv_std
        unit[...] = rows
        normed_all[z, core] = (rows * gain_in[...].reshape(1, W)).astype(BF16)
        normed_gather.start()

    def normed_done():
        normed_gather.finish()
        load_up.wait()

    def turn_normed():
        @pl.loop(0, 4)
        def _(m):
            for c in range(2):
                tokens = pl.ds(pl.multiple_of((m * 2 + c) * 128, 128), 128)
                normed_t[:, tokens] = jnp.transpose(normed_all[m, c])

    def unit_scatter1(i, order):
        slot = lax.rem(i, PAIRS)
        return (
            part.at[slot, order], land1.at[slot, order], s1.at[slot, order], v1.at[slot, order], order
        )

    def unit_scatter2(i, order):
        slot = lax.rem(i, PAIRS)
        return (
            part.at[slot, order], land2.at[slot, order], s2.at[slot, order], v2.at[slot, order], order, 32
        )

    def columns(p, order):
        return pl.ds(pl.multiple_of((p * 2 + order) * C, C), C)

    def multiply(i):
        slot = lax.rem(i, PAIRS)

        @pl.when(i < PAIRS)
        def _():
            for order in range(2):

                @pl.loop(0, 2)
                def _(n):
                    m = pl.ds(n * 2, 2)
                    value = dot_cols(ups_all[m].reshape(512, W), w_down[columns(i, order), :])
                    part[slot, order, m] = value.astype(BF16).reshape(2, 4, 64, C)

                scatter1(*unit_scatter1(i, order)).start()

        @pl.when(i >= PAIRS)
        def _():
            for order in range(2):

                @pl.loop(0, 2)
                def _(n):
                    m = pl.ds(n * 2, 2)
                    value = dot(normed_all[m].reshape(512, W), w_up[:, columns(i - PAIRS, order)])
                    part[slot, order, m] = value.astype(BF16).reshape(2, 4, 64, C)

                scatter1(*unit_scatter1(i, order)).start()

    def scatter1_middle(i):
        for order in range(2):
            scatter1(*unit_scatter1(i, order)).middle()

    def scatter1_finish(i):
        for order in range(2):
            scatter_turn(*unit_scatter1(i, order))
            scatter2(*unit_scatter2(i, order)).start()

    def scatter2_middle(i):
        for order in range(2):
            scatter2(*unit_scatter2(i, order)).middle()

    def pre_gather(p, order, stage):
        return (gather1, gather2)[stage](
            pre_grad.at[p, order], gs.at[p, order], gv.at[p, order], order
        )

    def act_gather(p, order, stage):
        return (gather1, gather2)[stage](
            act.at[p, order], asend.at[p, order], arecv.at[p, order], order
        )

    def scatter2_finish(i):
        slot = lax.rem(i, PAIRS)
        for order in range(2):
            halves = scatter2(*unit_scatter2(i, order)).finish()

            @pl.when(i < PAIRS)
            def _():
                for h in range(2):
                    act_grad[slot, order, pl.ds(h * 32, 32)] = halves[h]

            @pl.when(i >= PAIRS)
            def _():
                for h in range(2):
                    value, slope = gelu_parts(halves[h])
                    grad = act_grad[slot, order, pl.ds(h * 32, 32)] * slope
                    act[slot, order, x, y, pl.ds(h * 32, 32)] = value.astype(BF16)
                    pre_grad[slot, order, x, y, pl.ds(h * 32, 32)] = grad.astype(BF16)
                pre_gather(slot, order, 0).start()

    def gather_steps(make):
        def start(p):
            for order in range(2):
                make(p, order, 0).start()

        def middle1(p):
            for order in range(2):
                make(p, order, 0).middle()

        def turn(p):
            for order in range(2):
                one = make(p, order, 0)
                one.arrived()
                one.sent()
                make(p, order, 1).start()

        def middle2(p):
            for order in range(2):
                make(p, order, 1).middle()

        def finish(p):
            for order in range(2):
                one = make(p, order, 1)
                one.arrived()
                one.sent()

        return start, middle1, turn, middle2, finish

    _, pre_middle1, pre_turn, pre_middle2, pre_finish = gather_steps(pre_gather)
    act_start, act_middle1, act_turn, act_middle2, act_finish = gather_steps(act_gather)

    def up_store(p, order):
        slot = lax.rem(p, 2)
        return pltpu.make_async_copy(
            up_stage.at[slot, order], w_up_out.at[:, columns(p, order)], out_sem.at[0, slot, order]
        )

    def down_store(p, order):
        slot = lax.rem(p, 2)
        return pltpu.make_async_copy(
            down_stage.at[slot, order], w_down_out.at[columns(p, order), :], out_sem.at[1, slot, order]
        )

    def up_products(p):
        slot = lax.rem(p, 2)
        for order in range(2):

            @pl.when(p >= 2)
            def _():
                up_store(p - 2, order).wait()

            value = dot(normed_t[...], pre_grad[p, order].reshape(1024, C))
            up_stage[slot, order] = value.astype(BF16)

            up_store(p, order).start()

    def add_total(p):
        @pl.loop(0, 4)
        def _(m):
            value = dot_cols(pre_grad[p, 0, m].reshape(256, C), w_up[:, columns(p, 0)]) + dot_cols(
                pre_grad[p, 1, m].reshape(256, C), w_up[:, columns(p, 1)]
            )
            value = value.reshape(2, 128, W)

            @pl.when(p == 0)
            def _():
                total[m] = value

            @pl.when((p > 0) & (p < PAIRS - 1))
            def _():
                total[m] += value

            @pl.when(p == PAIRS - 1)
            def _():
                z_part[m] = (total[m] + value).astype(BF16)

        @pl.when(p == PAIRS - 1)
        def _():
            row_near().start()

    def act_products(p):
        slot = lax.rem(p, 2)
        for order in range(2):

            @pl.when(p >= 2)
            def _():
                down_store(p - 2, order).wait()

            for m in range(4):
                act_t[:, pl.ds(m * 256, 256)] = jnp.transpose(act[p, order, m].reshape(256, C))

            @pl.loop(0, 3)
            def _(n):
                cols = pl.ds(pl.multiple_of(n * 256, 256), 256)
                value = dot(act_t[...], ups_all[:, :, :, cols].reshape(1024, 256))
                down_stage[slot, order, :, cols] = value.astype(BF16)

            down_store(p, order).start()

    def gain_near():
        return remote(gain_sib.at[0], gain_sib.at[1], ggs.at[0], ggv.at[0], sibling)

    gain_far = Copies(
        lambda d: remote(
            gain_z.at[z], gain_z.at[z], ggs.at[1 + d], ggv.at[1 + d],
            ring_z.device(lax.rem(z + 1 + d, 4)),
        ),
        3,
    )

    def grad_sums():
        first, second = row_ring.finish()
        for h, share in enumerate((first, second)):
            total[0, 0, pl.ds(h * 64, 64)] = share
        grad = total[0, 0]
        aligned = grad * unit[...]
        scaled = grad * gain_in[...].reshape(1, W)
        stat_start(
            1, stat_x, ring_x,
            to_lanes(
                jnp.sum(scaled, axis=1, keepdims=True),
                jnp.sum(scaled * unit[...], axis=1, keepdims=True),
            ),
        )
        gain_sib[0] = jnp.broadcast_to(jnp.sum(aligned, axis=0, keepdims=True), (8, W))
        gain_near().start()

    def sums_x():
        stat_wait(1, stat_x, ring_x)
        stat_start(
            1, stat_y, ring_y, stat_x[1, 0] + stat_x[1, 1] + stat_x[1, 2] + stat_x[1, 3]
        )
        gain_near().wait_recv()
        gain_near().wait_send()
        gain_z[z] = gain_sib[0] + gain_sib[1]
        for copy in gain_far:
            copy.start()

    def grad_rows():
        stat_wait(1, stat_y, ring_y)
        means = (stat_y[1, 0] + stat_y[1, 1] + stat_y[1, 2] + stat_y[1, 3]) * (1.0 / D)
        scaled = total[0, 0] * gain_in[...].reshape(1, W)
        value = ups_in[...].astype(F32) + inv[:, 0:1] * (
            scaled - to_rows(means[0:1]) - unit[...] * to_rows(means[1:2])
        )
        rounded = value.astype(BF16)
        res_out[...] = rounded
        res_all[z, core] = rounded
        res_gather.start()

    def gain_done():
        for copy in gain_far:
            copy.wait_recv()
        for copy in gain_far:
            copy.wait_send()
        gain_out[...] = gain_z[0] + gain_z[1] + gain_z[2] + gain_z[3]

    def ctx_scatter1(order):
        return ctx_part.at[order], ctx_land1.at[order], c1s.at[order], c1v.at[order], order

    def ctx_scatter2(order):
        return ctx_part.at[order], ctx_land2.at[order], c2s.at[order], c2v.at[order], order, 32

    def context_product():
        res_gather.finish()
        for order in range(2):

            @pl.loop(0, 4)
            def _(m):
                value = dot_cols(
                    res_all[m].reshape(256, W), w_out_in[pl.ds(order * CH, CH), :]
                )
                ctx_part[order, m] = value.astype(BF16).reshape(4, 64, CH)

            scatter1(*ctx_scatter1(order)).start()

    def context_middle1():
        for order in range(2):
            scatter1(*ctx_scatter1(order)).middle()

    def context_turn():
        for order in range(2):
            scatter_turn(*ctx_scatter1(order))
            scatter2(*ctx_scatter2(order)).start()

    def context_middle2():
        for order in range(2):
            scatter2(*ctx_scatter2(order)).middle()

    def context_finish():
        for order in range(2):
            for h, share in enumerate(scatter2(*ctx_scatter2(order)).finish()):
                ctx_out[pl.ds(h * 32, 32), pl.ds(order * CH, CH)] = share.astype(BF16)

    def out_product(order):
        for n in range(3):
            cols = pl.ds(n * 256, 256)
            value = lax.dot_general(
                ctx_all[order].reshape(1024, CH),
                res_all[:, :, :, cols].reshape(1024, 256),
                (((0,), (0,)), ((), ())),
                preferred_element_type=F32,
            )
            w_out_out[pl.ds(order * CH, CH), cols] = value.astype(BF16)

    def out_first():
        out_product(0)

    def out_second():
        out_product(1)

    ups_all[z, core] = ups_in[...]
    ups_gather.start()
    for order in range(2):
        ctx_all[order, x, y] = ctx_in[:, pl.ds(order * CH, CH)]
        context_gather1(order).start()
    for order in range(2):
        context_gather1(order).middle()
    ups_gather.middle()
    for order in range(2):
        one = context_gather1(order)
        one.arrived()
        one.sent()
        context_gather2(order).start()
    ups_gather.last()
    for order in range(2):
        context_gather2(order).middle()
    ups_gather.finish()
    load_down.wait()

    def context_arrived():
        for order in range(2):
            one = context_gather2(order)
            one.arrived()
            one.sent()
        project_out()

    early = {
        1: [row_scatter_ring],
        2: [row_moments],
        3: [normalize],
        4: [normed_gather.last],
        20: [row_scatter_ring],
        21: [grad_sums],
        22: [grad_rows],
        23: [res_gather.last],
    }
    late = {
        0: [context_arrived],
        1: [row_ring.middle],
        2: [moments_x],
        3: [normed_gather.middle],
        5: [normed_done],
        7: [turn_normed],
        20: [row_ring.middle],
        21: [sums_x],
        22: [gain_done, res_gather.middle],
        23: [context_product],
        24: [context_middle1, out_first],
        25: [context_turn, out_second],
        26: [context_middle2],
        27: [context_finish],
    }
    base = PAIRS + 4
    act_base = base + ACT_DELAY
    steps = [
        (0, 2 * PAIRS, multiply),
        (1, 2 * PAIRS, scatter1_middle),
        (2, 2 * PAIRS, scatter1_finish),
        (3, 2 * PAIRS, scatter2_middle),
        (4, 2 * PAIRS, scatter2_finish),
        (base + 1, PAIRS, pre_middle1),
        (base + 2, PAIRS, pre_turn),
        (base + 3, PAIRS, pre_middle2),
        (base + 4, PAIRS, pre_finish),
        (base + 4, PAIRS, add_total),
        (act_base, PAIRS, act_start),
        (act_base + 1, PAIRS, act_middle1),
        (act_base + 2, PAIRS, act_turn),
        (act_base + 3, PAIRS, act_middle2),
        (act_base + 4, PAIRS, act_finish),
        None,
        (base + 4, PAIRS, up_products),
        (act_base + 4, PAIRS, act_products),
    ]

    def at_ticks(tick, events):
        for when, calls in events.items():

            @pl.when(tick == when)
            def _(calls=calls):
                for call in calls:
                    call()

    @pl.loop(0, TICKS)
    def _(tick):
        for entry in steps:
            if entry is None:
                at_ticks(tick, early)
                continue
            first, count, step = entry

            @pl.when((tick >= first) & (tick < first + count))
            def _(first=first, step=step):
                step(tick - first)

        at_ticks(tick, late)

    for p in (PAIRS - 2, PAIRS - 1):
        for order in range(2):
            up_store(p, order).wait()
            down_store(p, order).wait()


def on_device(context, residual, norm_gain, w_out, w_up, w_down, upstream):
    vmem = pl.BlockSpec(memory_space=pltpu.VMEM)
    hbm = pl.BlockSpec(memory_space=pl.ANY)
    shape = jax.ShapeDtypeStruct
    dma = pltpu.SemaphoreType.DMA
    outs = pl.pallas_call(
        kernel,
        out_shape=(
            shape((128, W), BF16),
            shape((64, W), BF16),
            shape((8, W), F32),
            shape((W, W), BF16),
            shape((W, 3072), BF16),
            shape((3072, W), BF16),
        ),
        in_specs=[vmem, vmem, vmem, vmem, hbm, hbm, vmem],
        out_specs=(vmem, vmem, vmem, vmem, hbm, hbm),
        scratch_shapes=[
            pltpu.VMEM((W, 3072), BF16),
            pltpu.VMEM((3072, W), BF16),
            pltpu.VMEM((PAIRS, 2, 4, 4, 64, C), BF16),
            pltpu.VMEM((PAIRS, 2, 6, 2, 64, C), BF16),
            pltpu.VMEM((PAIRS, 2, 6, 32, C), BF16),
            pltpu.VMEM((PAIRS, 2, 64, C), F32),
            pltpu.VMEM((PAIRS, 2, 4, 4, 64, C), BF16),
            pltpu.VMEM((PAIRS, 2, 4, 4, 64, C), BF16),
            pltpu.VMEM((2, 4, 4, 64, CH), BF16),
            pltpu.VMEM((2, 4, 4, 64, CH), BF16),
            pltpu.VMEM((2, 6, 2, 64, CH), BF16),
            pltpu.VMEM((2, 6, 32, CH), BF16),
            pltpu.VMEM((4, 2, 128, W), BF16),
            pltpu.VMEM((4, 2, 128, W), BF16),
            pltpu.VMEM((4, 2, 128, W), BF16),
            pltpu.VMEM((W, 1024), BF16),
            pltpu.VMEM((4, 2, 128, W), F32),
            pltpu.VMEM((4, 2, 128, W), BF16),
            pltpu.VMEM((4, 128, W), BF16),
            pltpu.VMEM((6, 64, W), BF16),
            pltpu.VMEM((2, 4, 8, 128), F32),
            pltpu.VMEM((2, 4, 8, 128), F32),
            pltpu.VMEM((128, W), F32),
            pltpu.VMEM((128, 128), F32),
            pltpu.VMEM((2, 8, W), F32),
            pltpu.VMEM((4, 8, W), F32),
            pltpu.VMEM((2, 2, W, C), BF16),
            pltpu.VMEM((2, 2, C, W), BF16),
            pltpu.VMEM((C, 1024), BF16),
            dma((2,)),
            dma((PAIRS, 2, 6)),
            dma((PAIRS, 2, 6)),
            dma((PAIRS, 2, 6)),
            dma((PAIRS, 2, 6)),
            dma((PAIRS, 2, 8)),
            dma((PAIRS, 2, 8)),
            dma((PAIRS, 2, 8)),
            dma((PAIRS, 2, 8)),
            dma((2, 12)),
            dma((2, 12)),
            dma((2, 6)),
            dma((2, 6)),
            dma((2, 6)),
            dma((2, 6)),
            dma((3, 10)),
            dma((3, 10)),
            dma((7,)),
            dma((7,)),
            dma((2, 6)),
            dma((2, 6)),
            dma((4,)),
            dma((4,)),
            dma((2, 2, 2)),
        ],
        compiler_params=pltpu.CompilerParams(
            collective_id=0, has_side_effects=True, vmem_limit_bytes=63 * 1024 * 1024
        ),
        cost_estimate=pl.CostEstimate(
            flops=28_000_000_000, bytes_accessed=25_000_000, transcendentals=200_000
        ),
    )(context, residual, norm_gain, w_out, w_up, w_down, upstream)
    return hand_over(outs)


def copy_kernel(*refs):
    ends, held, sems = refs[:10], refs[10:15], refs[15]
    parts = []
    for src, via, dst in zip(ends[:5], held, ends[5:]):
        rows = src.shape[0] // CUTS
        parts += [(src, via, dst, pl.ds(n * rows, rows)) for n in range(CUTS)]
    reads = [
        pltpu.make_async_copy(src.at[part], via.at[part], sems.at[0, n])
        for n, (src, via, _, part) in enumerate(parts)
    ]
    writes = [
        pltpu.make_async_copy(via.at[part], dst.at[part], sems.at[1, n])
        for n, (_, via, dst, part) in enumerate(parts)
    ]
    for copy in reads:
        copy.start()
    for n, copy in enumerate(writes):
        reads[n].wait()
        copy.start()
    for copy in writes:
        copy.wait()


def hand_over(outs):
    moved = [outs[n] for n in (0, 1, 3, 4, 5)]
    hbm = pl.BlockSpec(memory_space=pl.ANY)
    a, b, d, e, f = pl.pallas_call(
        copy_kernel,
        out_shape=[jax.ShapeDtypeStruct(ref.shape, ref.dtype) for ref in moved],
        in_specs=[hbm] * 5,
        out_specs=[hbm] * 5,
        scratch_shapes=[pltpu.VMEM(ref.shape, ref.dtype) for ref in moved]
        + [pltpu.SemaphoreType.DMA((2, 5 * CUTS))],
        compiler_params=pltpu.CompilerParams(vmem_limit_bytes=48 * 1024 * 1024),
        cost_estimate=pl.CostEstimate(flops=0, bytes_accessed=22_000_000, transcendentals=0),
    )(*moved)
    return a, b, outs[2][0], d, e, f


def solution(mesh):
    return jax.shard_map(
        on_device,
        mesh=mesh,
        in_specs=(
            P("col", "row"),
            P("row", "col"),
            P("col"),
            P("row", "col"),
            P("col", "row"),
            P("row", "col"),
            P("row", "col"),
        ),
        out_specs=(
            P("row", "col"),
            P("col", "row"),
            P("col"),
            P("row", "col"),
            P("col", "row"),
            P("row", "col"),
        ),
        check_vma=False,
    )
```

```python
import jax
import jax.numpy as jnp
from jax import lax
from jax.experimental import pallas as pl
from jax.experimental.pallas import tpu as pltpu
from jax.sharding import PartitionSpec as P

MESH = pl.DeviceIdType.MESH
BF16 = jnp.bfloat16
F32 = jnp.float32
D = 12288
W = 768
PAIRS = 6
C = 256
CH = 384
ACT_DELAY = 6
TICKS = 28
CUTS = 4


def gelu_parts(values):
    tanh_val = jnp.tanh(0.7978845608028654 * (values + 0.044715 * values * values * values))
    value = 0.5 * values * (1.0 + tanh_val)
    slope = 0.5 * (1.0 + tanh_val) + 0.5 * values * (
        1.0 - tanh_val * tanh_val
    ) * 0.7978845608028654 * (1.0 + 0.134145 * values * values)
    return value, slope


def dot(first_op, second_op):
    return jnp.dot(first_op, second_op, preferred_element_type=F32)


def dot_cols(first_op, second_op):
    return lax.dot_general(
        first_op, second_op, (((1,), (1,)), ((), ())), preferred_element_type=F32
    )


class Ring:
    def __init__(self, place, device):
        self.place = place
        self.right = lax.rem(place + 1, 4)
        self.opposite = lax.rem(place + 2, 4)
        self.left = lax.rem(place + 3, 4)
        self.device = device


def remote(src, dst, send, recv, device):
    return pltpu.make_async_remote_copy(
        src_ref=src, dst_ref=dst, send_sem=send, recv_sem=recv, device_id=device, device_id_type=MESH
    )


class Copies:
    def __init__(self, make, count):
        self.make, self.count = make, count

    def __getitem__(self, k):
        return self.make(k)

    def __iter__(self):
        return (self.make(k) for k in range(self.count))


class Scatter:
    def __init__(self, ring, half, landing, send, recv):
        r, l, o = ring.right, ring.left, ring.opposite
        plan = [(o, 0, r), (r, 1, r), (r, 0, r), (o, 1, l), (l, 0, l), (l, 1, l)]
        self.ring, self.half, self.landing = ring, half, landing

        def make(k):
            i, h, to = plan[k]
            return remote(half(i, h), landing.at[k], send.at[k], recv.at[k], ring.device(to))

        self.copies = Copies(make, 6)

    def start(self):
        for k in (0, 3, 1, 4):
            self.copies[k].start()

    def middle(self):
        for k, i, h, nxt in ((0, self.ring.right, 0, 2), (3, self.ring.left, 1, 5)):
            self.copies[k].wait_recv()
            part = self.half(i, h)
            part[...] = (part[...].astype(F32) + self.landing[k].astype(F32)).astype(BF16)
            self.copies[nxt].start()

    def finish(self):
        for k in (1, 4, 2, 5):
            self.copies[k].wait_recv()
        for copy in self.copies:
            copy.wait_send()
        me = self.ring.place
        first = (
            self.half(me, 0)[...].astype(F32)
            + self.landing[2].astype(F32)
            + self.landing[4].astype(F32)
        )
        second = (
            self.half(me, 1)[...].astype(F32)
            + self.landing[1].astype(F32)
            + self.landing[5].astype(F32)
        )
        return first, second


class Gather:
    def __init__(self, ring, group, half, send, recv):
        r, l = ring.right, ring.left
        me = ring.place

        def make(k):
            ref = (lambda: group(me), lambda: group(me), lambda: half(l, 0), lambda: half(r, 1))[k]()
            return remote(ref, ref, send.at[k], recv.at[k], ring.device((r, l, r, l)[k]))

        self.copies = Copies(make, 4)

    def start(self):
        self.copies[0].start()
        self.copies[1].start()

    def middle(self):
        self.copies[0].wait_recv()
        self.copies[2].start()
        self.copies[1].wait_recv()
        self.copies[3].start()

    def arrived(self):
        self.copies[2].wait_recv()
        self.copies[3].wait_recv()

    def sent(self):
        for copy in self.copies:
            copy.wait_send()


class HalfGather:
    def __init__(self, ring, half, send, recv):
        r, l, me = ring.right, ring.left, ring.place
        plan = [(me, 0, r), (me, 1, r), (me, 1, l), (me, 0, l), (l, 0, r), (r, 1, l)]

        def make(k):
            i, h, to = plan[k]
            return remote(half(i, h), half(i, h), send.at[k], recv.at[k], ring.device(to))

        self.copies = Copies(make, 6)

    def start(self):
        for k in (0, 2, 1, 3):
            self.copies[k].start()

    def middle(self):
        for first, forward in ((0, 4), (2, 5)):
            self.copies[first].wait_recv()
            self.copies[forward].start()
        for rest in (1, 3):
            self.copies[rest].wait_recv()

    def arrived(self):
        self.copies[4].wait_recv()
        self.copies[5].wait_recv()

    def sent(self):
        for copy in self.copies:
            copy.wait_send()


def grouped(ref, order, i, low, count):
    if order == 0:
        return ref.at[i, pl.ds(low, count)]
    return ref.at[pl.ds(low, count), i]


def block_of(ref, order, i, j):
    return ref.at[i, j] if order == 0 else ref.at[j, i]


def kernel(
    ctx_in, res_in, gain_in, w_out_in, w_up_hbm, w_down_hbm, ups_in,
    res_out, ctx_out, gain_out, w_out_out, w_up_out, w_down_out,
    w_up, w_down, part, land1, land2, act_grad, pre_grad, act,
    ctx_all, ctx_part, ctx_land1, ctx_land2, ups_all, normed_all, res_all, normed_t, total,
    z_part, z_sib, z_land, stat_x, stat_y, unit, inv, gain_sib, gain_z, up_stage, down_stage, act_t,
    w_sem, s1, v1, s2, v2, gs, gv, asend, arecv, cs, cv, c1s, c1v, c2s, c2v,
    zgs, zgv, zss, zsv, sts, stv, ggs, ggv, out_sem,
):
    row, col = lax.axis_index("row"), lax.axis_index("col")
    z, core = row // 2, lax.rem(row, 2)
    x, y = col // 4, lax.rem(col, 4)
    ring_x = Ring(x, lambda i: {"col": i * 4 + y})
    ring_y = Ring(y, lambda i: {"col": x * 4 + i})
    ring_z = Ring(z, lambda i: {"row": i * 2 + core})
    sibling = {"row": z * 2 + 1 - core}
    rings = (ring_x, ring_y)

    load_down = pltpu.make_async_copy(w_down_hbm, w_down, w_sem.at[0])
    load_up = pltpu.make_async_copy(w_up_hbm, w_up, w_sem.at[1])
    load_down.start()
    load_up.start()

    barrier = pltpu.get_barrier_semaphore()
    for ring in (ring_x, ring_y, ring_z):
        for i in (ring.left, ring.right, ring.opposite):
            pl.semaphore_signal(barrier, inc=1, device_id=ring.device(i), device_id_type=MESH)
    pl.semaphore_signal(barrier, inc=1, device_id=sibling, device_id_type=MESH)
    pl.semaphore_wait(barrier, 10)

    def scatter1(ref, landing, send, recv, order):
        ring = rings[order]
        return Scatter(ring, lambda i, h: grouped(ref, order, i, 2 * h, 2), landing, send, recv)

    def scatter2(ref, landing, send, recv, order, rows):
        mine, ring = rings[order].place, rings[1 - order]
        return Scatter(
            ring,
            lambda j, h: block_of(ref, order, mine, j).at[pl.ds(h * rows, rows)],
            landing, send, recv,
        )

    def gather1(ref, send, recv, order):
        mine, ring = rings[order].place, rings[1 - order]
        return Gather(
            ring,
            lambda j: block_of(ref, order, mine, j),
            lambda j, h: block_of(ref, order, mine, j).at[pl.ds(h * 32, 32)],
            send.at[pl.ds(0, 4)], recv.at[pl.ds(0, 4)],
        )

    def gather2(ref, send, recv, order):
        return Gather(
            rings[order],
            lambda i: grouped(ref, order, i, 0, 4),
            lambda i, h: grouped(ref, order, i, 2 * h, 2),
            send.at[pl.ds(4, 4)], recv.at[pl.ds(4, 4)],
        )

    def context_gather1(order):
        ref, mine = ctx_all.at[order], rings[order].place
        return HalfGather(
            rings[1 - order],
            lambda j, h: block_of(ref, order, mine, j).at[pl.ds(h * 32, 32)],
            cs.at[order, pl.ds(0, 6)], cv.at[order, pl.ds(0, 6)],
        )

    def context_gather2(order):
        return HalfGather(
            rings[order],
            lambda i, h: grouped(ctx_all.at[order], order, i, 2 * h, 2),
            cs.at[order, pl.ds(6, 6)], cv.at[order, pl.ds(6, 6)],
        )

    def scatter_turn(ref, landing, send, recv, order):
        one = scatter1(ref, landing, send, recv, order)
        first, second = one.finish()
        one.half(one.ring.place, 0)[...] = first.astype(BF16)
        one.half(one.ring.place, 1)[...] = second.astype(BF16)

    class RowGather:
        def __init__(self, ref, n):
            self.ring = HalfGather(
                ring_z,
                lambda i, h: ref.at[i, core, pl.ds(h * 64, 64)],
                zgs.at[n, pl.ds(0, 6)], zgv.at[n, pl.ds(0, 6)],
            )
            blocks = (z, ring_z.left, ring_z.right, ring_z.opposite)
            self.near = Copies(
                lambda k: remote(
                    ref.at[blocks[k], core], ref.at[blocks[k], core],
                    zgs.at[n, 6 + k], zgv.at[n, 6 + k], sibling,
                ),
                4,
            )

        def start(self):
            self.ring.start()
            self.near[0].start()

        def middle(self):
            self.ring.middle()
            self.near[1].start()
            self.near[2].start()

        def last(self):
            self.ring.arrived()
            self.near[3].start()

        def finish(self):
            for copy in self.near:
                copy.wait_recv()
            for copy in self.near:
                copy.wait_send()
            self.ring.sent()

    def row_near():
        return remote(z_part.at[:, 1 - core], z_sib, zss.at[6], zsv.at[6], sibling)

    row_ring = Scatter(
        ring_z, lambda i, h: z_part.at[i, core, pl.ds(h * 64, 64)], z_land, zss, zsv
    )

    def row_scatter_ring():
        row_near().wait_recv()
        row_near().wait_send()
        z_part[:, core] = (z_part[:, core].astype(F32) + z_sib[...].astype(F32)).astype(BF16)
        row_ring.start()

    def stat_copies(n, ref, ring):
        base = 0 if ref is stat_x else 3
        return Copies(
            lambda d: remote(
                ref.at[n, ring.place], ref.at[n, ring.place],
                sts.at[n, base + d], stv.at[n, base + d],
                ring.device(lax.rem(ring.place + 1 + d, 4)),
            ),
            3,
        )

    def to_lanes(first, second):
        lane = lax.broadcasted_iota(jnp.int32, (128, 128), 1)
        both = jnp.where(lane == 0, first, jnp.where(lane == 1, second, 0.0))
        return jnp.transpose(both)[0:8]

    def to_rows(values):
        return jnp.transpose(jnp.broadcast_to(values, (128, 128)))[:, 0:1]

    def stat_start(n, ref, ring, values):
        ref[n, ring.place] = values
        for copy in stat_copies(n, ref, ring):
            copy.start()

    def stat_wait(n, ref, ring):
        for copy in stat_copies(n, ref, ring):
            copy.wait_recv()
        for copy in stat_copies(n, ref, ring):
            copy.wait_send()

    def merge_moments(ref, count):
        means = [ref[0, i, 0:1] for i in range(4)]
        mean = (means[0] + means[1] + means[2] + means[3]) * 0.25
        squares = ref[0, 0, 1:2] + ref[0, 1, 1:2] + ref[0, 2, 1:2] + ref[0, 3, 1:2]
        for one in means:
            squares += count * (one - mean) * (one - mean)
        return mean, squares

    def two_rows(first, second):
        line = lax.broadcasted_iota(jnp.int32, (8, 128), 0)
        return jnp.where(line == 0, first, jnp.where(line == 1, second, 0.0))

    ups_gather, normed_gather, res_gather = (
        RowGather(ref, n) for n, ref in enumerate((ups_all, normed_all, res_all))
    )

    def project_out():
        @pl.loop(0, 4)
        def _(m):
            value = dot(ctx_all[0, m].reshape(256, CH), w_out_in[0:CH, :]) + dot(
                ctx_all[1, m].reshape(256, CH), w_out_in[CH:W, :]
            )
            z_part[m] = value.astype(BF16).reshape(2, 128, W)

        row_near().start()

    def row_moments():
        first, second = row_ring.finish()
        for h, share in enumerate((first, second)):
            unit[pl.ds(h * 64, 64)] = share + res_in[pl.ds(h * 64, 64)].astype(F32)
        summed = unit[...]
        mean = jnp.sum(summed, axis=1, keepdims=True) * (1.0 / W)
        centered = summed - mean
        squares = jnp.sum(centered * centered, axis=1, keepdims=True)
        stat_start(0, stat_x, ring_x, to_lanes(mean, squares))

    def moments_x():
        stat_wait(0, stat_x, ring_x)
        stat_start(0, stat_y, ring_y, two_rows(*merge_moments(stat_x, float(W))))

    def normalize():
        stat_wait(0, stat_y, ring_y)
        mean, squares = merge_moments(stat_y, float(4 * W))
        inv_row = lax.rsqrt(squares * (1.0 / D) + 1e-05)
        inv_std = to_rows(inv_row)
        inv[...] = jnp.broadcast_to(inv_std, (128, 128))
        rows = (unit[...] - to_rows(mean)) * inv_std
        unit[...] = rows
        normed_all[z, core] = (rows * gain_in[...].reshape(1, W)).astype(BF16)
        normed_gather.start()

    def normed_done():
        normed_gather.finish()
        load_up.wait()

    def turn_normed():
        @pl.loop(0, 4)
        def _(m):
            for c in range(2):
                tokens = pl.ds(pl.multiple_of((m * 2 + c) * 128, 128), 128)
                normed_t[:, tokens] = jnp.transpose(normed_all[m, c])

    def unit_scatter1(i, order):
        slot = lax.rem(i, PAIRS)
        return (
            part.at[slot, order], land1.at[slot, order], s1.at[slot, order], v1.at[slot, order], order
        )

    def unit_scatter2(i, order):
        slot = lax.rem(i, PAIRS)
        return (
            part.at[slot, order], land2.at[slot, order], s2.at[slot, order], v2.at[slot, order], order, 32
        )

    def columns(p, order):
        return pl.ds(pl.multiple_of((p * 2 + order) * C, C), C)

    def multiply(i):
        slot = lax.rem(i, PAIRS)

        @pl.when(i < PAIRS)
        def _():
            for order in range(2):

                @pl.loop(0, 2)
                def _(n):
                    m = pl.ds(n * 2, 2)
                    value = dot_cols(ups_all[m].reshape(512, W), w_down[columns(i, order), :])
                    part[slot, order, m] = value.astype(BF16).reshape(2, 4, 64, C)

                scatter1(*unit_scatter1(i, order)).start()

        @pl.when(i >= PAIRS)
        def _():
            for order in range(2):

                @pl.loop(0, 2)
                def _(n):
                    m = pl.ds(n * 2, 2)
                    value = dot(normed_all[m].reshape(512, W), w_up[:, columns(i - PAIRS, order)])
                    part[slot, order, m] = value.astype(BF16).reshape(2, 4, 64, C)

                scatter1(*unit_scatter1(i, order)).start()

    def scatter1_middle(i):
        for order in range(2):
            scatter1(*unit_scatter1(i, order)).middle()

    def scatter1_finish(i):
        for order in range(2):
            scatter_turn(*unit_scatter1(i, order))
            scatter2(*unit_scatter2(i, order)).start()

    def scatter2_middle(i):
        for order in range(2):
            scatter2(*unit_scatter2(i, order)).middle()

    def pre_gather(p, order, stage):
        return (gather1, gather2)[stage](
            pre_grad.at[p, order], gs.at[p, order], gv.at[p, order], order
        )

    def act_gather(p, order, stage):
        return (gather1, gather2)[stage](
            act.at[p, order], asend.at[p, order], arecv.at[p, order], order
        )

    def scatter2_finish(i):
        slot = lax.rem(i, PAIRS)
        for order in range(2):
            halves = scatter2(*unit_scatter2(i, order)).finish()

            @pl.when(i < PAIRS)
            def _():
                for h in range(2):
                    act_grad[slot, order, pl.ds(h * 32, 32)] = halves[h]

            @pl.when(i >= PAIRS)
            def _():
                for h in range(2):
                    value, slope = gelu_parts(halves[h])
                    grad = act_grad[slot, order, pl.ds(h * 32, 32)] * slope
                    act[slot, order, x, y, pl.ds(h * 32, 32)] = value.astype(BF16)
                    pre_grad[slot, order, x, y, pl.ds(h * 32, 32)] = grad.astype(BF16)
                pre_gather(slot, order, 0).start()

    def gather_steps(make):
        def start(p):
            for order in range(2):
                make(p, order, 0).start()

        def middle1(p):
            for order in range(2):
                make(p, order, 0).middle()

        def turn(p):
            for order in range(2):
                one = make(p, order, 0)
                one.arrived()
                one.sent()
                make(p, order, 1).start()

        def middle2(p):
            for order in range(2):
                make(p, order, 1).middle()

        def finish(p):
            for order in range(2):
                one = make(p, order, 1)
                one.arrived()
                one.sent()

        return start, middle1, turn, middle2, finish

    _, pre_middle1, pre_turn, pre_middle2, pre_finish = gather_steps(pre_gather)
    act_start, act_middle1, act_turn, act_middle2, act_finish = gather_steps(act_gather)

    def up_store(p, order):
        slot = lax.rem(p, 2)
        return pltpu.make_async_copy(
            up_stage.at[slot, order], w_up_out.at[:, columns(p, order)], out_sem.at[0, slot, order]
        )

    def down_store(p, order):
        slot = lax.rem(p, 2)
        return pltpu.make_async_copy(
            down_stage.at[slot, order], w_down_out.at[columns(p, order), :], out_sem.at[1, slot, order]
        )

    def up_products(p):
        slot = lax.rem(p, 2)
        for order in range(2):

            @pl.when(p >= 2)
            def _():
                up_store(p - 2, order).wait()

            value = dot(normed_t[...], pre_grad[p, order].reshape(1024, C))
            up_stage[slot, order] = value.astype(BF16)

            up_store(p, order).start()

    def add_total(p):
        @pl.loop(0, 4)
        def _(m):
            value = dot_cols(pre_grad[p, 0, m].reshape(256, C), w_up[:, columns(p, 0)]) + dot_cols(
                pre_grad[p, 1, m].reshape(256, C), w_up[:, columns(p, 1)]
            )
            value = value.reshape(2, 128, W)

            @pl.when(p == 0)
            def _():
                total[m] = value

            @pl.when((p > 0) & (p < PAIRS - 1))
            def _():
                total[m] += value

            @pl.when(p == PAIRS - 1)
            def _():
                z_part[m] = (total[m] + value).astype(BF16)

        @pl.when(p == PAIRS - 1)
        def _():
            row_near().start()

    def act_products(p):
        slot = lax.rem(p, 2)
        for order in range(2):

            @pl.when(p >= 2)
            def _():
                down_store(p - 2, order).wait()

            for m in range(4):
                act_t[:, pl.ds(m * 256, 256)] = jnp.transpose(act[p, order, m].reshape(256, C))

            @pl.loop(0, 3)
            def _(n):
                cols = pl.ds(pl.multiple_of(n * 256, 256), 256)
                value = dot(act_t[...], ups_all[:, :, :, cols].reshape(1024, 256))
                down_stage[slot, order, :, cols] = value.astype(BF16)

            down_store(p, order).start()

    def gain_near():
        return remote(gain_sib.at[0], gain_sib.at[1], ggs.at[0], ggv.at[0], sibling)

    gain_far = Copies(
        lambda d: remote(
            gain_z.at[z], gain_z.at[z], ggs.at[1 + d], ggv.at[1 + d],
            ring_z.device(lax.rem(z + 1 + d, 4)),
        ),
        3,
    )

    def grad_sums():
        first, second = row_ring.finish()
        for h, share in enumerate((first, second)):
            total[0, 0, pl.ds(h * 64, 64)] = share
        grad = total[0, 0]
        aligned = grad * unit[...]
        scaled = grad * gain_in[...].reshape(1, W)
        stat_start(
            1, stat_x, ring_x,
            to_lanes(
                jnp.sum(scaled, axis=1, keepdims=True),
                jnp.sum(scaled * unit[...], axis=1, keepdims=True),
            ),
        )
        gain_sib[0] = jnp.broadcast_to(jnp.sum(aligned, axis=0, keepdims=True), (8, W))
        gain_near().start()

    def sums_x():
        stat_wait(1, stat_x, ring_x)
        stat_start(
            1, stat_y, ring_y, stat_x[1, 0] + stat_x[1, 1] + stat_x[1, 2] + stat_x[1, 3]
        )
        gain_near().wait_recv()
        gain_near().wait_send()
        gain_z[z] = gain_sib[0] + gain_sib[1]
        for copy in gain_far:
            copy.start()

    def grad_rows():
        stat_wait(1, stat_y, ring_y)
        means = (stat_y[1, 0] + stat_y[1, 1] + stat_y[1, 2] + stat_y[1, 3]) * (1.0 / D)
        scaled = total[0, 0] * gain_in[...].reshape(1, W)
        value = ups_in[...].astype(F32) + inv[:, 0:1] * (
            scaled - to_rows(means[0:1]) - unit[...] * to_rows(means[1:2])
        )
        rounded = value.astype(BF16)
        res_out[...] = rounded
        res_all[z, core] = rounded
        res_gather.start()

    def gain_done():
        for copy in gain_far:
            copy.wait_recv()
        for copy in gain_far:
            copy.wait_send()
        gain_out[...] = gain_z[0] + gain_z[1] + gain_z[2] + gain_z[3]

    def ctx_scatter1(order):
        return ctx_part.at[order], ctx_land1.at[order], c1s.at[order], c1v.at[order], order

    def ctx_scatter2(order):
        return ctx_part.at[order], ctx_land2.at[order], c2s.at[order], c2v.at[order], order, 32

    def context_product():
        res_gather.finish()
        for order in range(2):

            @pl.loop(0, 4)
            def _(m):
                value = dot_cols(
                    res_all[m].reshape(256, W), w_out_in[pl.ds(order * CH, CH), :]
                )
                ctx_part[order, m] = value.astype(BF16).reshape(4, 64, CH)

            scatter1(*ctx_scatter1(order)).start()

    def context_middle1():
        for order in range(2):
            scatter1(*ctx_scatter1(order)).middle()

    def context_turn():
        for order in range(2):
            scatter_turn(*ctx_scatter1(order))
            scatter2(*ctx_scatter2(order)).start()

    def context_middle2():
        for order in range(2):
            scatter2(*ctx_scatter2(order)).middle()

    def context_finish():
        for order in range(2):
            for h, share in enumerate(scatter2(*ctx_scatter2(order)).finish()):
                ctx_out[pl.ds(h * 32, 32), pl.ds(order * CH, CH)] = share.astype(BF16)

    def out_product(order):
        for n in range(3):
            cols = pl.ds(n * 256, 256)
            value = lax.dot_general(
                ctx_all[order].reshape(1024, CH),
                res_all[:, :, :, cols].reshape(1024, 256),
                (((0,), (0,)), ((), ())),
                preferred_element_type=F32,
            )
            w_out_out[pl.ds(order * CH, CH), cols] = value.astype(BF16)

    def out_first():
        out_product(0)

    def out_second():
        out_product(1)

    ups_all[z, core] = ups_in[...]
    ups_gather.start()
    for order in range(2):
        ctx_all[order, x, y] = ctx_in[:, pl.ds(order * CH, CH)]
        context_gather1(order).start()
    for order in range(2):
        context_gather1(order).middle()
    ups_gather.middle()
    for order in range(2):
        one = context_gather1(order)
        one.arrived()
        one.sent()
        context_gather2(order).start()
    ups_gather.last()
    for order in range(2):
        context_gather2(order).middle()
    ups_gather.finish()
    load_down.wait()

    def context_arrived():
        for order in range(2):
            one = context_gather2(order)
            one.arrived()
            one.sent()
        project_out()

    early = {
        1: [row_scatter_ring],
        2: [row_moments],
        3: [normalize],
        4: [normed_gather.last],
        20: [row_scatter_ring],
        21: [grad_sums],
        22: [grad_rows],
        23: [res_gather.last],
    }
    late = {
        0: [context_arrived],
        1: [row_ring.middle],
        2: [moments_x],
        3: [normed_gather.middle],
        5: [normed_done],
        7: [turn_normed],
        20: [row_ring.middle],
        21: [sums_x],
        22: [gain_done, res_gather.middle],
        23: [context_product],
        24: [context_middle1, out_first],
        25: [context_turn, out_second],
        26: [context_middle2],
        27: [context_finish],
    }
    base = PAIRS + 4
    act_base = base + ACT_DELAY
    steps = [
        (0, 2 * PAIRS, multiply),
        (1, 2 * PAIRS, scatter1_middle),
        (2, 2 * PAIRS, scatter1_finish),
        (3, 2 * PAIRS, scatter2_middle),
        (4, 2 * PAIRS, scatter2_finish),
        (base + 1, PAIRS, pre_middle1),
        (base + 2, PAIRS, pre_turn),
        (base + 3, PAIRS, pre_middle2),
        (base + 4, PAIRS, pre_finish),
        (base + 4, PAIRS, add_total),
        (act_base, PAIRS, act_start),
        (act_base + 1, PAIRS, act_middle1),
        (act_base + 2, PAIRS, act_turn),
        (act_base + 3, PAIRS, act_middle2),
        (act_base + 4, PAIRS, act_finish),
        None,
        (base + 4, PAIRS, up_products),
        (act_base + 4, PAIRS, act_products),
    ]

    def at_ticks(tick, events):
        for when, calls in events.items():

            @pl.when(tick == when)
            def _(calls=calls):
                for call in calls:
                    call()

    @pl.loop(0, TICKS)
    def _(tick):
        for entry in steps:
            if entry is None:
                at_ticks(tick, early)
                continue
            first, count, step = entry

            @pl.when((tick >= first) & (tick < first + count))
            def _(first=first, step=step):
                step(tick - first)

        at_ticks(tick, late)

    for p in (PAIRS - 2, PAIRS - 1):
        for order in range(2):
            up_store(p, order).wait()
            down_store(p, order).wait()


def on_device(context, residual, norm_gain, w_out, w_up, w_down, upstream):
    vmem = pl.BlockSpec(memory_space=pltpu.VMEM)
    hbm = pl.BlockSpec(memory_space=pl.ANY)
    shape = jax.ShapeDtypeStruct
    dma = pltpu.SemaphoreType.DMA
    outs = pl.pallas_call(
        kernel,
        out_shape=(
            shape((128, W), BF16),
            shape((64, W), BF16),
            shape((8, W), F32),
            shape((W, W), BF16),
            shape((W, 3072), BF16),
            shape((3072, W), BF16),
        ),
        in_specs=[vmem, vmem, vmem, vmem, hbm, hbm, vmem],
        out_specs=(vmem, vmem, vmem, vmem, hbm, hbm),
        scratch_shapes=[
            pltpu.VMEM((W, 3072), BF16),
            pltpu.VMEM((3072, W), BF16),
            pltpu.VMEM((PAIRS, 2, 4, 4, 64, C), BF16),
            pltpu.VMEM((PAIRS, 2, 6, 2, 64, C), BF16),
            pltpu.VMEM((PAIRS, 2, 6, 32, C), BF16),
            pltpu.VMEM((PAIRS, 2, 64, C), F32),
            pltpu.VMEM((PAIRS, 2, 4, 4, 64, C), BF16),
            pltpu.VMEM((PAIRS, 2, 4, 4, 64, C), BF16),
            pltpu.VMEM((2, 4, 4, 64, CH), BF16),
            pltpu.VMEM((2, 4, 4, 64, CH), BF16),
            pltpu.VMEM((2, 6, 2, 64, CH), BF16),
            pltpu.VMEM((2, 6, 32, CH), BF16),
            pltpu.VMEM((4, 2, 128, W), BF16),
            pltpu.VMEM((4, 2, 128, W), BF16),
            pltpu.VMEM((4, 2, 128, W), BF16),
            pltpu.VMEM((W, 1024), BF16),
            pltpu.VMEM((4, 2, 128, W), F32),
            pltpu.VMEM((4, 2, 128, W), BF16),
            pltpu.VMEM((4, 128, W), BF16),
            pltpu.VMEM((6, 64, W), BF16),
            pltpu.VMEM((2, 4, 8, 128), F32),
            pltpu.VMEM((2, 4, 8, 128), F32),
            pltpu.VMEM((128, W), F32),
            pltpu.VMEM((128, 128), F32),
            pltpu.VMEM((2, 8, W), F32),
            pltpu.VMEM((4, 8, W), F32),
            pltpu.VMEM((2, 2, W, C), BF16),
            pltpu.VMEM((2, 2, C, W), BF16),
            pltpu.VMEM((C, 1024), BF16),
            dma((2,)),
            dma((PAIRS, 2, 6)),
            dma((PAIRS, 2, 6)),
            dma((PAIRS, 2, 6)),
            dma((PAIRS, 2, 6)),
            dma((PAIRS, 2, 8)),
            dma((PAIRS, 2, 8)),
            dma((PAIRS, 2, 8)),
            dma((PAIRS, 2, 8)),
            dma((2, 12)),
            dma((2, 12)),
            dma((2, 6)),
            dma((2, 6)),
            dma((2, 6)),
            dma((2, 6)),
            dma((3, 10)),
            dma((3, 10)),
            dma((7,)),
            dma((7,)),
            dma((2, 6)),
            dma((2, 6)),
            dma((4,)),
            dma((4,)),
            dma((2, 2, 2)),
        ],
        compiler_params=pltpu.CompilerParams(
            collective_id=0, has_side_effects=True, vmem_limit_bytes=63 * 1024 * 1024
        ),
        cost_estimate=pl.CostEstimate(
            flops=28_000_000_000, bytes_accessed=25_000_000, transcendentals=200_000
        ),
    )(context, residual, norm_gain, w_out, w_up, w_down, upstream)
    return hand_over(outs)


def copy_kernel(*refs):
    ends, held, sems = refs[:10], refs[10:15], refs[15]
    parts = []
    for src, via, dst in zip(ends[:5], held, ends[5:]):
        rows = src.shape[0] // CUTS
        parts += [(src, via, dst, pl.ds(n * rows, rows)) for n in range(CUTS)]
    reads = [
        pltpu.make_async_copy(src.at[part], via.at[part], sems.at[0, n])
        for n, (src, via, _, part) in enumerate(parts)
    ]
    writes = [
        pltpu.make_async_copy(via.at[part], dst.at[part], sems.at[1, n])
        for n, (_, via, dst, part) in enumerate(parts)
    ]
    for copy in reads:
        copy.start()
    for n, copy in enumerate(writes):
        reads[n].wait()
        copy.start()
    for copy in writes:
        copy.wait()


def hand_over(outs):
    moved = [outs[n] for n in (0, 1, 3, 4, 5)]
    hbm = pl.BlockSpec(memory_space=pl.ANY)
    a, b, d, e, f = pl.pallas_call(
        copy_kernel,
        out_shape=[jax.ShapeDtypeStruct(ref.shape, ref.dtype) for ref in moved],
        in_specs=[hbm] * 5,
        out_specs=[hbm] * 5,
        scratch_shapes=[pltpu.VMEM(ref.shape, ref.dtype) for ref in moved]
        + [pltpu.SemaphoreType.DMA((2, 5 * CUTS))],
        compiler_params=pltpu.CompilerParams(vmem_limit_bytes=63 * 1024 * 1024),
        cost_estimate=pl.CostEstimate(flops=0, bytes_accessed=22_000_000, transcendentals=0),
    )(*moved)
    return a, b, outs[2][0], d, e, f


def solution(mesh):
    return jax.shard_map(
        on_device,
        mesh=mesh,
        in_specs=(
            P("col", "row"),
            P("row", "col"),
            P("col"),
            P("row", "col"),
            P("col", "row"),
            P("row", "col"),
            P("row", "col"),
        ),
        out_specs=(
            P("row", "col"),
            P("col", "row"),
            P("col"),
            P("row", "col"),
            P("col", "row"),
            P("row", "col"),
        ),
        check_vma=False,
    )
```

```python
import jax
import jax.numpy as jnp
from jax import lax
from jax.experimental import pallas as pl
from jax.experimental.pallas import tpu as pltpu
from jax.sharding import PartitionSpec as P

MESH = pl.DeviceIdType.MESH
BF16 = jnp.bfloat16
F32 = jnp.float32
D = 12288
W = 768
PAIRS = 6
C = 256
CH = 384
ACT_DELAY = 6
TICKS = 28
CUTS = 4


def gelu_parts(values):
    tanh_val = jnp.tanh(0.7978845608028654 * (values + 0.044715 * values * values * values))
    value = 0.5 * values * (1.0 + tanh_val)
    slope = 0.5 * (1.0 + tanh_val) + 0.5 * values * (
        1.0 - tanh_val * tanh_val
    ) * 0.7978845608028654 * (1.0 + 0.134145 * values * values)
    return value, slope


def dot(first_op, second_op):
    return jnp.dot(first_op, second_op, preferred_element_type=F32)


def dot_cols(first_op, second_op):
    return lax.dot_general(
        first_op, second_op, (((1,), (1,)), ((), ())), preferred_element_type=F32
    )


class Ring:
    def __init__(self, place, device):
        self.place = place
        self.right = lax.rem(place + 1, 4)
        self.opposite = lax.rem(place + 2, 4)
        self.left = lax.rem(place + 3, 4)
        self.device = device


def remote(src, dst, send, recv, device):
    return pltpu.make_async_remote_copy(
        src_ref=src, dst_ref=dst, send_sem=send, recv_sem=recv, device_id=device, device_id_type=MESH
    )


class Copies:
    def __init__(self, make, count):
        self.make, self.count = make, count

    def __getitem__(self, k):
        return self.make(k)

    def __iter__(self):
        return (self.make(k) for k in range(self.count))


class Scatter:
    def __init__(self, ring, half, landing, send, recv):
        r, l, o = ring.right, ring.left, ring.opposite
        plan = [(o, 0, r), (r, 1, r), (r, 0, r), (o, 1, l), (l, 0, l), (l, 1, l)]
        self.ring, self.half, self.landing = ring, half, landing

        def make(k):
            i, h, to = plan[k]
            return remote(half(i, h), landing.at[k], send.at[k], recv.at[k], ring.device(to))

        self.copies = Copies(make, 6)

    def start(self):
        for k in (0, 3, 1, 4):
            self.copies[k].start()

    def middle(self):
        for k, i, h, nxt in ((0, self.ring.right, 0, 2), (3, self.ring.left, 1, 5)):
            self.copies[k].wait_recv()
            part = self.half(i, h)
            part[...] = (part[...].astype(F32) + self.landing[k].astype(F32)).astype(BF16)
            self.copies[nxt].start()

    def finish(self):
        for k in (1, 4, 2, 5):
            self.copies[k].wait_recv()
        for copy in self.copies:
            copy.wait_send()
        me = self.ring.place
        first = (
            self.half(me, 0)[...].astype(F32)
            + self.landing[2].astype(F32)
            + self.landing[4].astype(F32)
        )
        second = (
            self.half(me, 1)[...].astype(F32)
            + self.landing[1].astype(F32)
            + self.landing[5].astype(F32)
        )
        return first, second


class Gather:
    def __init__(self, ring, group, half, send, recv):
        r, l = ring.right, ring.left
        me = ring.place

        def make(k):
            ref = (lambda: group(me), lambda: group(me), lambda: half(l, 0), lambda: half(r, 1))[k]()
            return remote(ref, ref, send.at[k], recv.at[k], ring.device((r, l, r, l)[k]))

        self.copies = Copies(make, 4)

    def start(self):
        self.copies[0].start()
        self.copies[1].start()

    def middle(self):
        self.copies[0].wait_recv()
        self.copies[2].start()
        self.copies[1].wait_recv()
        self.copies[3].start()

    def arrived(self):
        self.copies[2].wait_recv()
        self.copies[3].wait_recv()

    def sent(self):
        for copy in self.copies:
            copy.wait_send()


class HalfGather:
    def __init__(self, ring, half, send, recv):
        r, l, me = ring.right, ring.left, ring.place
        plan = [(me, 0, r), (me, 1, r), (me, 1, l), (me, 0, l), (l, 0, r), (r, 1, l)]

        def make(k):
            i, h, to = plan[k]
            return remote(half(i, h), half(i, h), send.at[k], recv.at[k], ring.device(to))

        self.copies = Copies(make, 6)

    def start(self):
        for k in (0, 2, 1, 3):
            self.copies[k].start()

    def middle(self):
        for first, forward in ((0, 4), (2, 5)):
            self.copies[first].wait_recv()
            self.copies[forward].start()
        for rest in (1, 3):
            self.copies[rest].wait_recv()

    def arrived(self):
        self.copies[4].wait_recv()
        self.copies[5].wait_recv()

    def sent(self):
        for copy in self.copies:
            copy.wait_send()


def grouped(ref, order, i, low, count):
    if order == 0:
        return ref.at[i, pl.ds(low, count)]
    return ref.at[pl.ds(low, count), i]


def block_of(ref, order, i, j):
    return ref.at[i, j] if order == 0 else ref.at[j, i]


def kernel(
    ctx_in, res_in, gain_in, w_out_in, w_up_hbm, w_down_hbm, ups_in,
    res_out, ctx_out, gain_out, w_out_out, w_up_out, w_down_out,
    w_up, w_down, part, land1, land2, act_grad, pre_grad, act,
    ctx_all, ctx_part, ctx_land1, ctx_land2, ups_all, normed_all, res_all, normed_t, total,
    z_part, z_sib, z_land, stat_x, stat_y, unit, inv, gain_sib, gain_z, up_stage, down_stage, act_t,
    w_sem, s1, v1, s2, v2, gs, gv, asend, arecv, cs, cv, c1s, c1v, c2s, c2v,
    zgs, zgv, zss, zsv, sts, stv, ggs, ggv, out_sem,
):
    row, col = lax.axis_index("row"), lax.axis_index("col")
    z, core = row // 2, lax.rem(row, 2)
    x, y = col // 4, lax.rem(col, 4)
    ring_x = Ring(x, lambda i: {"col": i * 4 + y})
    ring_y = Ring(y, lambda i: {"col": x * 4 + i})
    ring_z = Ring(z, lambda i: {"row": i * 2 + core})
    sibling = {"row": z * 2 + 1 - core}
    rings = (ring_x, ring_y)

    load_down = pltpu.make_async_copy(w_down_hbm, w_down, w_sem.at[0])
    load_up = pltpu.make_async_copy(w_up_hbm, w_up, w_sem.at[1])
    load_down.start()
    load_up.start()

    barrier = pltpu.get_barrier_semaphore()
    for ring in (ring_x, ring_y, ring_z):
        for i in (ring.left, ring.right, ring.opposite):
            pl.semaphore_signal(barrier, inc=1, device_id=ring.device(i), device_id_type=MESH)
    pl.semaphore_signal(barrier, inc=1, device_id=sibling, device_id_type=MESH)
    pl.semaphore_wait(barrier, 10)

    def scatter1(ref, landing, send, recv, order):
        ring = rings[order]
        return Scatter(ring, lambda i, h: grouped(ref, order, i, 2 * h, 2), landing, send, recv)

    def scatter2(ref, landing, send, recv, order, rows):
        mine, ring = rings[order].place, rings[1 - order]
        return Scatter(
            ring,
            lambda j, h: block_of(ref, order, mine, j).at[pl.ds(h * rows, rows)],
            landing, send, recv,
        )

    def gather1(ref, send, recv, order):
        mine, ring = rings[order].place, rings[1 - order]
        return Gather(
            ring,
            lambda j: block_of(ref, order, mine, j),
            lambda j, h: block_of(ref, order, mine, j).at[pl.ds(h * 32, 32)],
            send.at[pl.ds(0, 4)], recv.at[pl.ds(0, 4)],
        )

    def gather2(ref, send, recv, order):
        return Gather(
            rings[order],
            lambda i: grouped(ref, order, i, 0, 4),
            lambda i, h: grouped(ref, order, i, 2 * h, 2),
            send.at[pl.ds(4, 4)], recv.at[pl.ds(4, 4)],
        )

    def context_gather1(order):
        ref, mine = ctx_all.at[order], rings[order].place
        return HalfGather(
            rings[1 - order],
            lambda j, h: block_of(ref, order, mine, j).at[pl.ds(h * 32, 32)],
            cs.at[order, pl.ds(0, 6)], cv.at[order, pl.ds(0, 6)],
        )

    def context_gather2(order):
        return HalfGather(
            rings[order],
            lambda i, h: grouped(ctx_all.at[order], order, i, 2 * h, 2),
            cs.at[order, pl.ds(6, 6)], cv.at[order, pl.ds(6, 6)],
        )

    def scatter_turn(ref, landing, send, recv, order):
        one = scatter1(ref, landing, send, recv, order)
        first, second = one.finish()
        one.half(one.ring.place, 0)[...] = first.astype(BF16)
        one.half(one.ring.place, 1)[...] = second.astype(BF16)

    class RowGather:
        def __init__(self, ref, n):
            self.ring = HalfGather(
                ring_z,
                lambda i, h: ref.at[i, core, pl.ds(h * 64, 64)],
                zgs.at[n, pl.ds(0, 6)], zgv.at[n, pl.ds(0, 6)],
            )
            blocks = (z, ring_z.left, ring_z.right, ring_z.opposite)
            self.near = Copies(
                lambda k: remote(
                    ref.at[blocks[k], core], ref.at[blocks[k], core],
                    zgs.at[n, 6 + k], zgv.at[n, 6 + k], sibling,
                ),
                4,
            )

        def start(self):
            self.ring.start()
            self.near[0].start()

        def middle(self):
            self.ring.middle()
            self.near[1].start()
            self.near[2].start()

        def last(self):
            self.ring.arrived()
            self.near[3].start()

        def finish(self):
            for copy in self.near:
                copy.wait_recv()
            for copy in self.near:
                copy.wait_send()
            self.ring.sent()

    def row_near():
        return remote(z_part.at[:, 1 - core], z_sib, zss.at[6], zsv.at[6], sibling)

    row_ring = Scatter(
        ring_z, lambda i, h: z_part.at[i, core, pl.ds(h * 64, 64)], z_land, zss, zsv
    )

    def row_scatter_ring():
        row_near().wait_recv()
        row_near().wait_send()
        z_part[:, core] = (z_part[:, core].astype(F32) + z_sib[...].astype(F32)).astype(BF16)
        row_ring.start()

    def stat_copies(n, ref, ring):
        base = 0 if ref is stat_x else 3
        return Copies(
            lambda d: remote(
                ref.at[n, ring.place], ref.at[n, ring.place],
                sts.at[n, base + d], stv.at[n, base + d],
                ring.device(lax.rem(ring.place + 1 + d, 4)),
            ),
            3,
        )

    def to_lanes(first, second):
        lane = lax.broadcasted_iota(jnp.int32, (128, 128), 1)
        both = jnp.where(lane == 0, first, jnp.where(lane == 1, second, 0.0))
        return jnp.transpose(both)[0:8]

    def to_rows(values):
        return jnp.transpose(jnp.broadcast_to(values, (128, 128)))[:, 0:1]

    def stat_start(n, ref, ring, values):
        ref[n, ring.place] = values
        for copy in stat_copies(n, ref, ring):
            copy.start()

    def stat_wait(n, ref, ring):
        for copy in stat_copies(n, ref, ring):
            copy.wait_recv()
        for copy in stat_copies(n, ref, ring):
            copy.wait_send()

    def merge_moments(ref, count):
        means = [ref[0, i, 0:1] for i in range(4)]
        mean = (means[0] + means[1] + means[2] + means[3]) * 0.25
        squares = ref[0, 0, 1:2] + ref[0, 1, 1:2] + ref[0, 2, 1:2] + ref[0, 3, 1:2]
        for one in means:
            squares += count * (one - mean) * (one - mean)
        return mean, squares

    def two_rows(first, second):
        line = lax.broadcasted_iota(jnp.int32, (8, 128), 0)
        return jnp.where(line == 0, first, jnp.where(line == 1, second, 0.0))

    ups_gather, normed_gather, res_gather = (
        RowGather(ref, n) for n, ref in enumerate((ups_all, normed_all, res_all))
    )

    def project_out():
        @pl.loop(0, 4)
        def _(m):
            value = dot(ctx_all[0, m].reshape(256, CH), w_out_in[0:CH, :]) + dot(
                ctx_all[1, m].reshape(256, CH), w_out_in[CH:W, :]
            )
            z_part[m] = value.astype(BF16).reshape(2, 128, W)

        row_near().start()

    def row_moments():
        first, second = row_ring.finish()
        for h, share in enumerate((first, second)):
            unit[pl.ds(h * 64, 64)] = share + res_in[pl.ds(h * 64, 64)].astype(F32)
        summed = unit[...]
        mean = jnp.sum(summed, axis=1, keepdims=True) * (1.0 / W)
        centered = summed - mean
        squares = jnp.sum(centered * centered, axis=1, keepdims=True)
        stat_start(0, stat_x, ring_x, to_lanes(mean, squares))

    def moments_x():
        stat_wait(0, stat_x, ring_x)
        stat_start(0, stat_y, ring_y, two_rows(*merge_moments(stat_x, float(W))))

    def normalize():
        stat_wait(0, stat_y, ring_y)
        mean, squares = merge_moments(stat_y, float(4 * W))
        inv_row = lax.rsqrt(squares * (1.0 / D) + 1e-05)
        inv_std = to_rows(inv_row)
        inv[...] = jnp.broadcast_to(inv_std, (128, 128))
        rows = (unit[...] - to_rows(mean)) * inv_std
        unit[...] = rows
        normed_all[z, core] = (rows * gain_in[...].reshape(1, W)).astype(BF16)
        normed_gather.start()

    def normed_done():
        normed_gather.finish()
        load_up.wait()

    def turn_normed():
        @pl.loop(0, 4)
        def _(m):
            for c in range(2):
                tokens = pl.ds(pl.multiple_of((m * 2 + c) * 128, 128), 128)
                normed_t[:, tokens] = jnp.transpose(normed_all[m, c])

    def unit_scatter1(i, order):
        slot = lax.rem(i, PAIRS)
        return (
            part.at[slot, order], land1.at[slot, order], s1.at[slot, order], v1.at[slot, order], order
        )

    def unit_scatter2(i, order):
        slot = lax.rem(i, PAIRS)
        return (
            part.at[slot, order], land2.at[slot, order], s2.at[slot, order], v2.at[slot, order], order, 32
        )

    def columns(p, order):
        return pl.ds(pl.multiple_of((p * 2 + order) * C, C), C)

    def multiply(i):
        slot = lax.rem(i, PAIRS)

        @pl.when(i < PAIRS)
        def _():
            for order in range(2):

                @pl.loop(0, 2)
                def _(n):
                    m = pl.ds(n * 2, 2)
                    value = dot_cols(ups_all[m].reshape(512, W), w_down[columns(i, order), :])
                    part[slot, order, m] = value.astype(BF16).reshape(2, 4, 64, C)

                scatter1(*unit_scatter1(i, order)).start()

        @pl.when(i >= PAIRS)
        def _():
            for order in range(2):

                @pl.loop(0, 2)
                def _(n):
                    m = pl.ds(n * 2, 2)
                    value = dot(normed_all[m].reshape(512, W), w_up[:, columns(i - PAIRS, order)])
                    part[slot, order, m] = value.astype(BF16).reshape(2, 4, 64, C)

                scatter1(*unit_scatter1(i, order)).start()

    def scatter1_middle(i):
        for order in range(2):
            scatter1(*unit_scatter1(i, order)).middle()

    def scatter1_finish(i):
        for order in range(2):
            scatter_turn(*unit_scatter1(i, order))
            scatter2(*unit_scatter2(i, order)).start()

    def scatter2_middle(i):
        for order in range(2):
            scatter2(*unit_scatter2(i, order)).middle()

    def pre_gather(p, order, stage):
        return (gather1, gather2)[stage](
            pre_grad.at[p, order], gs.at[p, order], gv.at[p, order], order
        )

    def act_gather(p, order, stage):
        return (gather1, gather2)[stage](
            act.at[p, order], asend.at[p, order], arecv.at[p, order], order
        )

    def scatter2_finish(i):
        slot = lax.rem(i, PAIRS)
        for order in range(2):
            halves = scatter2(*unit_scatter2(i, order)).finish()

            @pl.when(i < PAIRS)
            def _():
                for h in range(2):
                    act_grad[slot, order, pl.ds(h * 32, 32)] = halves[h]

            @pl.when(i >= PAIRS)
            def _():
                for h in range(2):
                    value, slope = gelu_parts(halves[h])
                    grad = act_grad[slot, order, pl.ds(h * 32, 32)] * slope
                    act[slot, order, x, y, pl.ds(h * 32, 32)] = value.astype(BF16)
                    pre_grad[slot, order, x, y, pl.ds(h * 32, 32)] = grad.astype(BF16)
                pre_gather(slot, order, 0).start()

    def gather_steps(make):
        def start(p):
            for order in range(2):
                make(p, order, 0).start()

        def middle1(p):
            for order in range(2):
                make(p, order, 0).middle()

        def turn(p):
            for order in range(2):
                one = make(p, order, 0)
                one.arrived()
                one.sent()
                make(p, order, 1).start()

        def middle2(p):
            for order in range(2):
                make(p, order, 1).middle()

        def finish(p):
            for order in range(2):
                one = make(p, order, 1)
                one.arrived()
                one.sent()

        return start, middle1, turn, middle2, finish

    _, pre_middle1, pre_turn, pre_middle2, pre_finish = gather_steps(pre_gather)
    act_start, act_middle1, act_turn, act_middle2, act_finish = gather_steps(act_gather)

    def up_store(p, order):
        slot = lax.rem(p, 2)
        return pltpu.make_async_copy(
            up_stage.at[slot, order], w_up_out.at[:, columns(p, order)], out_sem.at[0, slot, order]
        )

    def down_store(p, order):
        slot = lax.rem(p, 2)
        return pltpu.make_async_copy(
            down_stage.at[slot, order], w_down_out.at[columns(p, order), :], out_sem.at[1, slot, order]
        )

    def up_products(p):
        slot = lax.rem(p, 2)
        for order in range(2):

            @pl.when(p >= 2)
            def _():
                up_store(p - 2, order).wait()

            value = dot(normed_t[...], pre_grad[p, order].reshape(1024, C))
            up_stage[slot, order] = value.astype(BF16)

            up_store(p, order).start()

    def add_total(p):
        @pl.loop(0, 4)
        def _(m):
            value = dot_cols(pre_grad[p, 0, m].reshape(256, C), w_up[:, columns(p, 0)]) + dot_cols(
                pre_grad[p, 1, m].reshape(256, C), w_up[:, columns(p, 1)]
            )
            value = value.reshape(2, 128, W)

            @pl.when(p == 0)
            def _():
                total[m] = value

            @pl.when((p > 0) & (p < PAIRS - 1))
            def _():
                total[m] += value

            @pl.when(p == PAIRS - 1)
            def _():
                z_part[m] = (total[m] + value).astype(BF16)

        @pl.when(p == PAIRS - 1)
        def _():
            row_near().start()

    def act_products(p):
        slot = lax.rem(p, 2)
        for order in range(2):

            @pl.when(p >= 2)
            def _():
                down_store(p - 2, order).wait()

            for m in range(4):
                act_t[:, pl.ds(m * 256, 256)] = jnp.transpose(act[p, order, m].reshape(256, C))

            @pl.loop(0, 3)
            def _(n):
                cols = pl.ds(pl.multiple_of(n * 256, 256), 256)
                value = dot(act_t[...], ups_all[:, :, :, cols].reshape(1024, 256))
                down_stage[slot, order, :, cols] = value.astype(BF16)

            down_store(p, order).start()

    def gain_near():
        return remote(gain_sib.at[0], gain_sib.at[1], ggs.at[0], ggv.at[0], sibling)

    gain_far = Copies(
        lambda d: remote(
            gain_z.at[z], gain_z.at[z], ggs.at[1 + d], ggv.at[1 + d],
            ring_z.device(lax.rem(z + 1 + d, 4)),
        ),
        3,
    )

    def grad_sums():
        first, second = row_ring.finish()
        for h, share in enumerate((first, second)):
            total[0, 0, pl.ds(h * 64, 64)] = share
        grad = total[0, 0]
        aligned = grad * unit[...]
        scaled = grad * gain_in[...].reshape(1, W)
        stat_start(
            1, stat_x, ring_x,
            to_lanes(
                jnp.sum(scaled, axis=1, keepdims=True),
                jnp.sum(scaled * unit[...], axis=1, keepdims=True),
            ),
        )
        gain_sib[0] = jnp.broadcast_to(jnp.sum(aligned, axis=0, keepdims=True), (8, W))
        gain_near().start()

    def sums_x():
        stat_wait(1, stat_x, ring_x)
        stat_start(
            1, stat_y, ring_y, stat_x[1, 0] + stat_x[1, 1] + stat_x[1, 2] + stat_x[1, 3]
        )
        gain_near().wait_recv()
        gain_near().wait_send()
        gain_z[z] = gain_sib[0] + gain_sib[1]
        for copy in gain_far:
            copy.start()

    def grad_rows():
        stat_wait(1, stat_y, ring_y)
        means = (stat_y[1, 0] + stat_y[1, 1] + stat_y[1, 2] + stat_y[1, 3]) * (1.0 / D)
        scaled = total[0, 0] * gain_in[...].reshape(1, W)
        value = ups_in[...].astype(F32) + inv[:, 0:1] * (
            scaled - to_rows(means[0:1]) - unit[...] * to_rows(means[1:2])
        )
        rounded = value.astype(BF16)
        res_out[...] = rounded
        res_all[z, core] = rounded
        res_gather.start()

    def gain_done():
        for copy in gain_far:
            copy.wait_recv()
        for copy in gain_far:
            copy.wait_send()
        gain_out[...] = gain_z[0] + gain_z[1] + gain_z[2] + gain_z[3]

    def ctx_scatter1(order):
        return ctx_part.at[order], ctx_land1.at[order], c1s.at[order], c1v.at[order], order

    def ctx_scatter2(order):
        return ctx_part.at[order], ctx_land2.at[order], c2s.at[order], c2v.at[order], order, 32

    def context_product():
        res_gather.finish()
        for order in range(2):

            @pl.loop(0, 4)
            def _(m):
                value = dot_cols(
                    res_all[m].reshape(256, W), w_out_in[pl.ds(order * CH, CH), :]
                )
                ctx_part[order, m] = value.astype(BF16).reshape(4, 64, CH)

            scatter1(*ctx_scatter1(order)).start()

    def context_middle1():
        for order in range(2):
            scatter1(*ctx_scatter1(order)).middle()

    def context_turn():
        for order in range(2):
            scatter_turn(*ctx_scatter1(order))
            scatter2(*ctx_scatter2(order)).start()

    def context_middle2():
        for order in range(2):
            scatter2(*ctx_scatter2(order)).middle()

    def context_finish():
        for order in range(2):
            for h, share in enumerate(scatter2(*ctx_scatter2(order)).finish()):
                ctx_out[pl.ds(h * 32, 32), pl.ds(order * CH, CH)] = share.astype(BF16)

    def out_product(order):
        for n in range(3):
            cols = pl.ds(n * 256, 256)
            value = lax.dot_general(
                ctx_all[order].reshape(1024, CH),
                res_all[:, :, :, cols].reshape(1024, 256),
                (((0,), (0,)), ((), ())),
                preferred_element_type=F32,
            )
            w_out_out[pl.ds(order * CH, CH), cols] = value.astype(BF16)

    def out_first():
        out_product(0)

    def out_second():
        out_product(1)

    ups_all[z, core] = ups_in[...]
    ups_gather.start()
    for order in range(2):
        ctx_all[order, x, y] = ctx_in[:, pl.ds(order * CH, CH)]
        context_gather1(order).start()
    for order in range(2):
        context_gather1(order).middle()
    ups_gather.middle()
    for order in range(2):
        one = context_gather1(order)
        one.arrived()
        one.sent()
        context_gather2(order).start()
    ups_gather.last()
    for order in range(2):
        context_gather2(order).middle()
    ups_gather.finish()
    load_down.wait()

    def context_arrived():
        for order in range(2):
            one = context_gather2(order)
            one.arrived()
            one.sent()
        project_out()

    early = {
        1: [row_scatter_ring],
        2: [row_moments],
        3: [normalize],
        4: [normed_gather.last],
        20: [row_scatter_ring],
        21: [grad_sums],
        22: [grad_rows],
        23: [res_gather.last],
    }
    late = {
        0: [context_arrived],
        1: [row_ring.middle],
        2: [moments_x],
        3: [normed_gather.middle],
        5: [normed_done],
        7: [turn_normed],
        20: [row_ring.middle],
        21: [sums_x],
        22: [gain_done, res_gather.middle],
        23: [context_product],
        24: [context_middle1, out_first],
        25: [context_turn, out_second],
        26: [context_middle2],
        27: [context_finish],
    }
    base = PAIRS + 4
    act_base = base + ACT_DELAY
    steps = [
        (0, 2 * PAIRS, multiply),
        (1, 2 * PAIRS, scatter1_middle),
        (2, 2 * PAIRS, scatter1_finish),
        (3, 2 * PAIRS, scatter2_middle),
        (4, 2 * PAIRS, scatter2_finish),
        (base + 1, PAIRS, pre_middle1),
        (base + 2, PAIRS, pre_turn),
        (base + 3, PAIRS, pre_middle2),
        (base + 4, PAIRS, pre_finish),
        (base + 4, PAIRS, add_total),
        (act_base, PAIRS, act_start),
        (act_base + 1, PAIRS, act_middle1),
        (act_base + 2, PAIRS, act_turn),
        (act_base + 3, PAIRS, act_middle2),
        (act_base + 4, PAIRS, act_finish),
        None,
        (base + 4, PAIRS, up_products),
        (act_base + 4, PAIRS, act_products),
    ]

    def at_ticks(tick, events):
        for when, calls in events.items():

            @pl.when(tick == when)
            def _(calls=calls):
                for call in calls:
                    call()

    @pl.loop(0, TICKS)
    def _(tick):
        for entry in steps:
            if entry is None:
                at_ticks(tick, early)
                continue
            first, count, step = entry

            @pl.when((tick >= first) & (tick < first + count))
            def _(first=first, step=step):
                step(tick - first)

        at_ticks(tick, late)

    for p in (PAIRS - 2, PAIRS - 1):
        for order in range(2):
            up_store(p, order).wait()
            down_store(p, order).wait()


def on_device(context, residual, norm_gain, w_out, w_up, w_down, upstream):
    vmem = pl.BlockSpec(memory_space=pltpu.VMEM)
    hbm = pl.BlockSpec(memory_space=pl.ANY)
    shape = jax.ShapeDtypeStruct
    dma = pltpu.SemaphoreType.DMA
    outs = pl.pallas_call(
        kernel,
        out_shape=(
            shape((128, W), BF16),
            shape((64, W), BF16),
            shape((8, W), F32),
            shape((W, W), BF16),
            shape((W, 3072), BF16),
            shape((3072, W), BF16),
        ),
        in_specs=[vmem, vmem, vmem, vmem, hbm, hbm, vmem],
        out_specs=(vmem, vmem, vmem, vmem, hbm, hbm),
        scratch_shapes=[
            pltpu.VMEM((W, 3072), BF16),
            pltpu.VMEM((3072, W), BF16),
            pltpu.VMEM((PAIRS, 2, 4, 4, 64, C), BF16),
            pltpu.VMEM((PAIRS, 2, 6, 2, 64, C), BF16),
            pltpu.VMEM((PAIRS, 2, 6, 32, C), BF16),
            pltpu.VMEM((PAIRS, 2, 64, C), F32),
            pltpu.VMEM((PAIRS, 2, 4, 4, 64, C), BF16),
            pltpu.VMEM((PAIRS, 2, 4, 4, 64, C), BF16),
            pltpu.VMEM((2, 4, 4, 64, CH), BF16),
            pltpu.VMEM((2, 4, 4, 64, CH), BF16),
            pltpu.VMEM((2, 6, 2, 64, CH), BF16),
            pltpu.VMEM((2, 6, 32, CH), BF16),
            pltpu.VMEM((4, 2, 128, W), BF16),
            pltpu.VMEM((4, 2, 128, W), BF16),
            pltpu.VMEM((4, 2, 128, W), BF16),
            pltpu.VMEM((W, 1024), BF16),
            pltpu.VMEM((4, 2, 128, W), F32),
            pltpu.VMEM((4, 2, 128, W), BF16),
            pltpu.VMEM((4, 128, W), BF16),
            pltpu.VMEM((6, 64, W), BF16),
            pltpu.VMEM((2, 4, 8, 128), F32),
            pltpu.VMEM((2, 4, 8, 128), F32),
            pltpu.VMEM((128, W), F32),
            pltpu.VMEM((128, 128), F32),
            pltpu.VMEM((2, 8, W), F32),
            pltpu.VMEM((4, 8, W), F32),
            pltpu.VMEM((2, 2, W, C), BF16),
            pltpu.VMEM((2, 2, C, W), BF16),
            pltpu.VMEM((C, 1024), BF16),
            dma((2,)),
            dma((PAIRS, 2, 6)),
            dma((PAIRS, 2, 6)),
            dma((PAIRS, 2, 6)),
            dma((PAIRS, 2, 6)),
            dma((PAIRS, 2, 8)),
            dma((PAIRS, 2, 8)),
            dma((PAIRS, 2, 8)),
            dma((PAIRS, 2, 8)),
            dma((2, 12)),
            dma((2, 12)),
            dma((2, 6)),
            dma((2, 6)),
            dma((2, 6)),
            dma((2, 6)),
            dma((3, 10)),
            dma((3, 10)),
            dma((7,)),
            dma((7,)),
            dma((2, 6)),
            dma((2, 6)),
            dma((4,)),
            dma((4,)),
            dma((2, 2, 2)),
        ],
        compiler_params=pltpu.CompilerParams(
            collective_id=0, has_side_effects=True, vmem_limit_bytes=63 * 1024 * 1024
        ),
        cost_estimate=pl.CostEstimate(
            flops=28_000_000_000, bytes_accessed=25_000_000, transcendentals=200_000
        ),
    )(context, residual, norm_gain, w_out, w_up, w_down, upstream)
    return hand_over(outs)


def copy_kernel(*refs):
    ends, gain, held, sems = refs[:5] + refs[6:11], (refs[5], refs[11]), refs[12:17], refs[17]
    parts = []
    for src, via, dst in zip(ends[:5], held, ends[5:]):
        rows = src.shape[0] // CUTS
        parts += [(src, via, dst, pl.ds(n * rows, rows)) for n in range(CUTS)]
    reads = [
        pltpu.make_async_copy(src.at[part], via.at[part], sems.at[0, n])
        for n, (src, via, _, part) in enumerate(parts)
    ]
    writes = [
        pltpu.make_async_copy(via.at[part], dst.at[part], sems.at[1, n])
        for n, (_, via, dst, part) in enumerate(parts)
    ]
    for copy in reads:
        copy.start()
    gain[1][...] = gain[0][0:1, :].reshape(W)
    for n, copy in enumerate(writes):
        reads[n].wait()
        copy.start()
    for copy in writes:
        copy.wait()


def hand_over(outs):
    moved = [outs[n] for n in (0, 1, 3, 4, 5)]
    hbm = pl.BlockSpec(memory_space=pl.ANY)
    vmem = pl.BlockSpec(memory_space=pltpu.VMEM)
    a, b, d, e, f, gain = pl.pallas_call(
        copy_kernel,
        out_shape=[jax.ShapeDtypeStruct(ref.shape, ref.dtype) for ref in moved]
        + [jax.ShapeDtypeStruct((W,), F32)],
        in_specs=[hbm] * 5 + [vmem],
        out_specs=[hbm] * 5 + [vmem],
        scratch_shapes=[pltpu.VMEM(ref.shape, ref.dtype) for ref in moved]
        + [pltpu.SemaphoreType.DMA((2, 5 * CUTS))],
        compiler_params=pltpu.CompilerParams(vmem_limit_bytes=63 * 1024 * 1024),
        cost_estimate=pl.CostEstimate(flops=0, bytes_accessed=22_000_000, transcendentals=0),
    )(*moved, outs[2])
    return a, b, gain, d, e, f


def solution(mesh):
    return jax.shard_map(
        on_device,
        mesh=mesh,
        in_specs=(
            P("col", "row"),
            P("row", "col"),
            P("col"),
            P("row", "col"),
            P("col", "row"),
            P("row", "col"),
            P("row", "col"),
        ),
        out_specs=(
            P("row", "col"),
            P("col", "row"),
            P("col"),
            P("row", "col"),
            P("col", "row"),
            P("row", "col"),
        ),
        check_vma=False,
    )
```
